128 devices in a mesh: block: 32 (over z, y, x_hi), slab: 2 (over core), event: 2 (over x_lo).
Axes of the slice: x: 4 (x_hi: 2, x_lo: 2; x = x_hi * 2 + x_lo), y: 4, z: 4, core: 2. Of those that a mesh axis runs over, the one named last changes fastest.
Arguments:
- adjoint_start: float32 [4, 1024, 32, 512], P('event', 'block', 'slab'), may hold values from -3 to 3
- velocity_start: float32 [4, 1024, 32, 512], P('event', 'block', 'slab'), may hold values from -3 to 3
- source_field: float32 [4, 1024, 32, 512], P('event', 'block', 'slab'), may hold values from -6 to 6
- source_time: float32 [4, 4], P('event'), may hold values from -4 to 4
- modulus: float32 [1024, 32, 512], P('block', 'slab'), may hold values from 1 to 4
- inverse_mass: float32 [1024, 32, 512], P('block', 'slab'), may hold values from 1 to 3
- crust_depth: int32 [1024, 512], P('block'), may hold values from 1 to 8
Outputs:
- adjoint_end: float32 [4, 1024, 32, 512], P('event', 'block', 'slab')
- hessian: float32 [1024, 32, 512], P('block', 'slab')
The draws below stay inside these ranges and needn't reach their ends.
All inputs are finite; a program needn't handle non-finite values.
Results may differ from the reference program's by a relative error of at most 0.0001.
Values sent between devices are 32-bit elements; how exact they have to be, the bound alone decides.
A program may use at most 128 MiB of HBM per device.

```python
import math
import jax
import jax.numpy as jnp
import numpy as np
from jax import lax

STEPS = 4
PXT = 1024
PZT = 32
PY = 512
EVENTS = 4
CRUST = 8


def plant(result, key, least, largest):
    longest = result.shape.index(max(result.shape))
    spots = []
    for shift in (0, 1):
        where = [jax.random.randint(jax.random.fold_in(key, axis), (), 0, length) for axis, length in enumerate(result.shape)]
        where[longest] = (where[longest] + shift) % result.shape[longest]
        spots.append(tuple(where))
    return result.at[spots[0]].set(least).at[spots[1]].set(largest)


def steps_of(rng, extent, shards, least, largest):
    factor_of, own = 1.0, jax.random.fold_in(rng, 6)
    for dim, shards_of in shards:
        heights = jnp.exp(jax.random.uniform(jax.random.fold_in(own, dim), (shards_of,), jnp.float32, least / len(shards), largest / len(shards)))
        factor_of = factor_of * jnp.repeat(heights, extent[dim] // shards_of).reshape([-1 if axis == dim else 1 for axis in range(len(extent))])
    return factor_of


def normal_values(rng, extent, spread, limit, pieces=(), kind=jnp.bfloat16):
    gain = steps_of(rng, extent, pieces, -0.22, 0.18) if pieces else 1.0
    entries = jax.random.normal(rng, extent, jnp.float32) * spread * gain
    return jnp.minimum(jnp.maximum(entries, -limit), limit).astype(kind)


def setup_inputs(seed: int = 0) -> dict:
    streams_of = jax.random.split(jax.random.key(seed), 8)
    adjoint_start = normal_values(streams_of[0], (EVENTS, PXT, PZT, PY), 0.5, 3.0, ((0, 2), (1, 32), (2, 2)), jnp.float32)
    velocity_start = normal_values(streams_of[1], (EVENTS, PXT, PZT, PY), 0.5, 3.0, ((0, 2), (1, 32), (2, 2)), jnp.float32)
    source_field = normal_values(streams_of[2], (EVENTS, PXT, PZT, PY), 1.0, 6.0, ((0, 2), (1, 32), (2, 2)), jnp.float32)
    source_time = normal_values(streams_of[3], (EVENTS, STEPS), 1.0, 4.0, ((0, 2),), jnp.float32)
    modulus = jnp.clip(jnp.exp(math.log(4.0) - 1.3862944 * jax.random.uniform(streams_of[4], (PXT, PZT, PY), jnp.float32) ** steps_of(streams_of[4], (PXT, PZT, PY), ((0, 32), (1, 2)), -0.2, 0.2)), 1.0, 4.0)
    inverse_mass = jnp.clip(jnp.exp(math.log(3.0) - 1.0986123 * jax.random.uniform(streams_of[5], (PXT, PZT, PY), jnp.float32) ** steps_of(streams_of[5], (PXT, PZT, PY), ((0, 32), (1, 2)), -0.2, 0.2)), 1.0, 3.0)
    crust_depth = plant(jax.random.randint(streams_of[6], (PXT, PY), 1, CRUST + 1), jax.random.fold_in(streams_of[6], 1), 1, CRUST).astype(jnp.int32)
    return {"adjoint_start": adjoint_start, "velocity_start": velocity_start, "source_field": source_field, "source_time": source_time, "modulus": modulus, "inverse_mass": inverse_mass, "crust_depth": crust_depth}


GLL_WEIGHTS = (0.1, 49.0 / 90.0, 32.0 / 45.0, 49.0 / 90.0, 0.1)
TIME_STEP = 0.1
CRUST_FACTOR = 0.35

def derivative_table():
    points = np.array([-1.0, -np.sqrt(3.0 / 7.0), 0.0, np.sqrt(3.0 / 7.0), 1.0])
    scales = np.array([np.prod([points[one] - points[other] for other in range(5) if other != one]) for one in range(5)])
    table = np.zeros((5, 5))
    for target in range(5):
        for anchor in range(5):
            if target != anchor:
                table[target, anchor] = scales[target] / (scales[anchor] * (points[target] - points[anchor]))
        table[target, target] = -np.sum(table[target])
    return table

def assembled_weights(start, count, free_end):
    position = start + jnp.arange(count, dtype=jnp.int32)
    remainder = position % 4
    weights = jnp.where(remainder == 0, 0.2, jnp.where(remainder == 2, 32.0 / 45.0, 49.0 / 90.0)).astype(jnp.float32)
    if free_end:
        weights = jnp.where(position == 0, 0.1, weights).astype(jnp.float32)
    return weights

def node_values(values_in, axis):
    elements = (values_in.shape[axis] - 1) // 4
    return [lax.slice_in_dim(values_in, offset, offset + 4 * (elements - 1) + 1, 4, axis) for offset in range(5)]

def node_coefs(extended, axis, outer_weights):
    picked = node_values(extended, axis)
    return [GLL_WEIGHTS[inner] * picked[inner] * outer_weights for inner in range(5)]

def element_term(values_in, coefs, axis):
    table = derivative_table()
    picked = node_values(values_in, axis)
    scaled = []
    for inner in range(5):
        slope = sum((float(table[inner, outer]) * picked[outer] for outer in range(5)))
        scaled.append(coefs[inner] * slope)
    parts = [sum((float(table[inner, outer]) * scaled[inner] for inner in range(5))) for outer in range(5)]
    elements = parts[0].shape[axis]
    carried = lax.slice_in_dim(parts[4], 0, elements - 1, 1, axis)
    zero_layer = jnp.zeros_like(lax.slice_in_dim(parts[4], 0, 1, 1, axis))
    first_part = parts[0] + jnp.concatenate([zero_layer, carried], axis)
    stacked = jnp.stack([first_part, parts[1], parts[2], parts[3]], axis + 1)
    shape_out = parts[0].shape[:axis] + (4 * elements,) + parts[0].shape[axis + 1:]
    interior = stacked.reshape(shape_out)
    extra = lax.slice_in_dim(parts[4], elements - 1, elements, 1, axis)
    return (interior, extra)

def reference(adjoint_start, velocity_start, source_field, source_time, modulus, inverse_mass, crust_depth):
    depth_index = jnp.arange(PZT, dtype=jnp.int32)
    crust = depth_index[None, :, None] >= (PZT - crust_depth)[:, None, :]
    stiffness = jnp.where(crust, CRUST_FACTOR * modulus, modulus)
    weight_x = assembled_weights(0, PXT, False)
    weight_z = assembled_weights(0, PZT, True)
    weight_y = assembled_weights(0, PY, True)
    along_x = jnp.concatenate([stiffness, stiffness[:1]], 0)
    coef_x = node_coefs(along_x, 0, weight_z[:, None] * weight_y[None, :])
    along_z = jnp.concatenate([stiffness, jnp.zeros((PXT, 1, PY), jnp.float32)], 1)
    coef_z = node_coefs(along_z, 1, weight_x[:, None, None] * weight_y[None, None, :])
    along_y = jnp.concatenate([stiffness, jnp.zeros((PXT, PZT, 1), jnp.float32)], 2)
    coef_y = node_coefs(along_y, 2, weight_x[:, None, None] * weight_z[None, :, None])

    def apply_operator(values_in):
        interior, extra = element_term(jnp.concatenate([values_in, values_in[:1]], 0), coef_x, 0)
        part_x = interior.at[0:1].add(extra)
        part_z, dropped_z = element_term(jnp.concatenate([values_in, jnp.zeros((PXT, 1, PY), jnp.float32)], 1), coef_z, 1)
        part_y, dropped_y = element_term(jnp.concatenate([values_in, jnp.zeros((PXT, PZT, 1), jnp.float32)], 2), coef_y, 2)
        return part_x + part_z + part_y

    def one_event(inputs):
        displacement, velocity, source, time_values = inputs
        kernel = jnp.zeros_like(displacement)
        for step_index in range(STEPS):
            forcing = time_values[step_index] * source - apply_operator(displacement)
            acceleration = inverse_mass * forcing
            velocity = velocity + TIME_STEP * acceleration
            displacement = displacement + TIME_STEP * velocity
            velocity_kick = TIME_STEP * acceleration
            kernel = kernel + velocity_kick * velocity_kick
        return (displacement, kernel)
    finals, kernels = lax.map(one_event, (adjoint_start, velocity_start, source_field, source_time))
    hessian = lax.optimization_barrier(jnp.sum(kernels, 0)) / (EVENTS * STEPS)
    return (finals, hessian)
```

```python
import functools

import jax
import jax.numpy as jnp
import numpy as np
from jax import lax
from jax.experimental import pallas as pl
from jax.experimental.pallas import tpu as pltpu
from jax.sharding import PartitionSpec as P

STEPS = 4
TIME_STEP = 0.1
CRUST_FACTOR = 0.35
WEIGHTS = (0.1, 49.0 / 90.0, 32.0 / 45.0, 49.0 / 90.0, 0.1)
ASSEMBLED = (0.2, 49.0 / 90.0, 32.0 / 45.0, 49.0 / 90.0)
MESH = pl.DeviceIdType.MESH
TILE = (8, 128)


def derivative_table():
    points = np.array([-1.0, -np.sqrt(3.0 / 7.0), 0.0, np.sqrt(3.0 / 7.0), 1.0])
    scales = np.array(
        [
            np.prod([points[one] - points[other] for other in range(5) if other != one])
            for one in range(5)
        ]
    )
    table = np.zeros((5, 5))
    for target in range(5):
        for anchor in range(5):
            if target != anchor:
                table[target, anchor] = scales[target] / (
                    scales[anchor] * (points[target] - points[anchor])
                )
        table[target, target] = -np.sum(table[target])
    return table


D = derivative_table()
A4, B4 = (D[4, 4] - D[4, 0]) / 2, (D[4, 3] - D[4, 1]) / 2
E4, T4 = (D[4, 4] + D[4, 0]) / 2, (D[4, 3] + D[4, 1]) / 2
A3, B3 = (D[3, 4] - D[3, 0]) / 2, (D[3, 3] - D[3, 1]) / 2
E3, T3 = (D[3, 4] + D[3, 0]) / 2, (D[3, 3] + D[3, 1]) / 2
SCALE = (A4, A3, D[2, 3], A3, A4)
DN = D / np.array(SCALE)[:, None]
KAPPA0, GAMMA, DELTA = B4 / A4, E4 / A4, T4 / A4
KAPPA1, EPSILON, ZETA = B3 / A3, E3 / A3, T3 / A3
KAPPA2 = D[2, 4] / D[2, 3]
RHO = [WEIGHTS[i] * SCALE[i] ** 2 for i in range(5)]


def line(u0, u1, u2, u3, u4, c0, c1, c2, c3, c4, last=True):
    a, b = u4 - u0, u3 - u1
    twice = u2 + u2
    e, f = (u4 + u0) - twice, (u3 + u1) - twice
    p, q = a + KAPPA0 * b, GAMMA * e + DELTA * f
    r, s = a + KAPPA1 * b, EPSILON * e + ZETA * f
    h4, h0 = (p + q) * c4, (p - q) * c0
    h3, h1 = (r + s) * c3, (r - s) * c1
    h2 = (b + KAPPA2 * a) * c2
    hp, hm = h4 + h0, h4 - h0
    ep, em = h3 + h1, h3 - h1
    fa = (hp + ep) + KAPPA2 * h2
    fb = (KAPPA0 * hp + KAPPA1 * ep) + h2
    fe = GAMMA * hm + EPSILON * em
    ff = DELTA * hm + ZETA * em
    total = fe + ff
    return fe - fa, ff - fb, total + total, ff + fb, (fe + fa if last else None)


def body(slabs, blocks, *refs):
    (
        start_hbm, velocity_hbm, source_hbm, time_ref, modulus_hbm, mass_hbm, crust_hbm,
        end_hbm, hessian_hbm,
        nat_u, nat_v, nat_s, nat_g, nat_m, nat_c,
        u, w, sf, im, hs, gx, gy, gz, gy4, gz4, kx, kdx, kz, kdz, ub, pb, fs,
        zs, zh, gzs, gzh, layer, crust, sent, got, index,
        in_sem, out_sem, zsend, zrecv, usend, urecv, psend, precv, qsend, qrecv, hsend, hrecv,
    ) = refs
    block = lax.axis_index("block")
    slab = lax.axis_index("slab")
    event = lax.axis_index("event")
    before = (lax.rem(block + blocks - 1, blocks), slab, event)
    after = (lax.rem(block + 1, blocks), slab, event)
    other_slab = (block, 1 - slab, event)
    other_event = (block, slab, 1 - event)

    barrier = pltpu.get_barrier_semaphore()
    for device in (before, after, other_slab, other_event):
        pl.semaphore_signal(barrier, inc=1, device_id=device, device_id_type=MESH)

    def loads(j):
        at = pl.ds(4 * j, 4)
        pairs = []
        for k in range(4):
            lanes = (slice(None), pl.ds(128 * k, 128))
            pairs.append((modulus_hbm.at[at, *lanes], nat_g.at[k, at]))
            pairs.append((mass_hbm.at[at, *lanes], nat_m.at[k, at]))
            for e in range(2):
                pairs.append((start_hbm.at[e, at, *lanes], nat_u.at[k, at, e]))
                pairs.append((source_hbm.at[e, at, *lanes], nat_s.at[k, at, e]))
                pairs.append((velocity_hbm.at[e, at, *lanes], nat_v.at[k, at, e]))
        return [
            pltpu.make_async_copy(source, target, in_sem.at[j, k])
            for k, (source, target) in enumerate(pairs)
        ]

    crust_load = pltpu.make_async_copy(crust_hbm, nat_c, in_sem.at[8, 0])
    crust_load.start()

    @pl.loop(0, 8)
    def _(n):
        for copy in loads(lax.rem(7 * n, 8)):
            copy.start()

    lane = lax.broadcasted_iota(jnp.int32, TILE, 1)
    row = lax.broadcasted_iota(jnp.int32, TILE, 0)
    radial = row & 3
    for r in range(4):
        index[r] = 4 * (lane & 31) + ((r - (lane >> 5)) & 3)
        index[4 + r] = 32 * ((r - (lane & 3)) & 3) + (lane >> 2)
    bit0, bit1 = (lane & 1) == 1, (lane & 2) == 2
    block0, block1 = (lane & 32) == 32, (lane & 64) == 64
    upper = row < 4
    is0 = jnp.where(slab == 0, 1.0, 0.0).astype(jnp.float32)
    is1 = 1.0 - is0

    def gather(value, k):
        return jnp.take_along_axis(value, index[k], axis=1)

    def apart(t):
        x = [jnp.where(bit0, t[(r + 3) % 4], t[r]) for r in range(4)]
        m = [jnp.where(bit1, x[(r + 2) % 4], x[r]) for r in range(4)]
        n = [gather(m[r], r) for r in range(4)]
        y = [jnp.where(block0, n[(k + 1) % 4], n[k]) for k in range(4)]
        return [jnp.where(block1, y[(k + 2) % 4], y[k]) for k in range(4)]

    def together(o):
        y = [jnp.where(block0, o[(r + 3) % 4], o[r]) for r in range(4)]
        n = [jnp.where(block1, y[(r + 2) % 4], y[r]) for r in range(4)]
        m = [gather(n[r], 4 + r) for r in range(4)]
        z = [jnp.where(bit0, m[(k + 1) % 4], m[k]) for k in range(4)]
        return [jnp.where(bit1, z[(k + 2) % 4], z[k]) for k in range(4)]

    def turn(value, shift):
        return value if shift % 8 == 0 else pltpu.roll(value, shift % 8, 0)

    def pack(values, at):
        result = turn(values[0], -at)
        for k in range(1, 4):
            result = jnp.where(radial == k, turn(values[k], k - at), result)
        return result

    def twice_events(value):
        other = pltpu.roll(value, 4, 0)
        return jnp.where(upper, value, other), jnp.where(upper, other, value)

    rows_u = nat_u.reshape(4 * 1024, 128)
    rows_v = nat_v.reshape(4 * 1024, 128)
    rows_s = nat_s.reshape(4 * 1024, 128)
    rows_g = nat_g.reshape(4 * 512, 128)
    rows_m = nat_m.reshape(4 * 512, 128)
    rows_sent = sent.reshape(4 * 512, 128)

    def strided(ref, first):
        count = ref.shape[0] // 4
        return [ref[pl.ds(first + count * k, 8, stride=4), :] for k in range(4)]

    edge_z = jnp.where(slab == 0, jnp.where(radial == 0, 0.1, 0.2), 0.2).astype(jnp.float32)
    edge_y = jnp.where(lane == 0, 0.1, 0.2).astype(jnp.float32)
    weight_z = [edge_z] + [jnp.float32(ASSEMBLED[k]) for k in range(1, 4)]
    weight_y = [edge_y] + [jnp.float32(ASSEMBLED[k]) for k in range(1, 4)]

    crust_load.wait()

    @pl.loop(0, 4)
    def _(part):
        got_rows = apart(
            [nat_c[pl.ds(pl.multiple_of(8 * part, 8), 8), pl.ds(128 * k, 128)] for k in range(4)]
        )
        for k in range(4):
            crust[k, pl.ds(pl.multiple_of(8 * part, 8), 8), :] = got_rows[k]

    def set_up(j):
        for copy in loads(j):
            copy.wait()

        @pl.loop(0, 4)
        def _(zm):
            for half in range(2):
                x = 4 * j + 2 * half
                moduli = apart(strided(rows_g, 16 * x + zm))
                masses = apart(strided(rows_m, 16 * x + zm))
                place = slab * 16 + 4 * radial + zm
                az = jnp.where(
                    zm == 0, edge_z, jnp.where(zm == 2, ASSEMBLED[2], ASSEMBLED[1])
                ).astype(jnp.float32)
                rho_z = jnp.where(
                    zm == 0, RHO[0], jnp.where(zm == 2, RHO[2], RHO[1])
                ).astype(jnp.float32)
                for ym in range(4):
                    depth = jnp.where(
                        upper,
                        jnp.broadcast_to(crust[ym, pl.ds(x, 1), :], TILE),
                        jnp.broadcast_to(crust[ym, pl.ds(x + 1, 1), :], TILE),
                    )
                    stiff = jnp.where(
                        place >= 16 * slabs - depth, CRUST_FACTOR * moduli[ym], moduli[ym]
                    )
                    mass = masses[ym] * (TIME_STEP * TIME_STEP)
                    at = 4 * zm + ym
                    for side, (value, small) in enumerate(
                        zip(twice_events(stiff), twice_events(mass))
                    ):
                        xm = 2 * half + side
                        in_y, in_z = value * weight_y[ym], value * az
                        gx[x + side, at] = in_y * az * RHO[xm]
                        gy[x + side, at] = in_z * (RHO[ym] * ASSEMBLED[xm])
                        gz[x + side, at] = in_y * (rho_z * ASSEMBLED[xm])
                        im[x + side, at] = small
            for xm in range(4):
                x = 4 * j + xm
                values = apart(strided(rows_u, 32 * x + zm))
                for ym in range(4):
                    u[x, 4 * zm + ym] = values[ym]
                values = apart(strided(rows_v, 32 * x + zm))
                for ym in range(4):
                    w[x, 4 * zm + ym] = values[ym] * TIME_STEP
                values = apart(strided(rows_s, 32 * x + zm))
                for ym in range(4):
                    sf[x, 4 * zm + ym] = values[ym] * im[x, 4 * zm + ym]
                    hs[x, 4 * zm + ym] = jnp.zeros(TILE, jnp.float32)
                gy4[x, zm] = jnp.where(lane == 127, 0.0, pltpu.roll(gy[x, 4 * zm], 127, 1))
            for ym in range(4):
                ub[0, j, 4 * zm + ym] = u[4 * j, 4 * zm + ym]

        @pl.loop(0, 4)
        def _(xm):
            x = 4 * j + xm
            first = pack([gz[x, ym] for ym in range(4)], 0)
            ends = [pack([gz[x, 4 * zm + ym] for ym in range(4)], 3) for zm in range(4)]
            total = ends[0] * float(DN[0, 4] ** 2)
            for zm in range(1, 4):
                total = total + ends[zm] * float(DN[zm, 4] ** 2)
            for zm in range(4):
                kz[x, zm] = ends[zm]
            gzs[x] = is0 * total + is1 * first

    def gz_copy(j):
        at = pl.ds(4 * j, 4)
        return pltpu.make_async_remote_copy(
            src_ref=gzs.at[at], dst_ref=gzh.at[at], send_sem=zsend.at[4, j], recv_sem=zrecv.at[4, j],
            device_id=other_slab, device_id_type=MESH,
        )

    def z_copy(t, j):
        at = pl.ds(4 * j, 4)
        return pltpu.make_async_remote_copy(
            src_ref=zs.at[t, at], dst_ref=zh.at[t, at], send_sem=zsend.at[t, j], recv_sem=zrecv.at[t, j],
            device_id=other_slab, device_id_type=MESH,
        )

    def u_copy(t):
        return pltpu.make_async_remote_copy(
            src_ref=ub.at[t, 0], dst_ref=ub.at[t, 8], send_sem=usend.at[t], recv_sem=urecv.at[t],
            device_id=before, device_id_type=MESH,
        )

    def g_copy():
        return pltpu.make_async_remote_copy(
            src_ref=gx.at[0], dst_ref=gx.at[32], send_sem=usend.at[4], recv_sem=urecv.at[4],
            device_id=before, device_id_type=MESH,
        )

    def p_copy(t):
        return pltpu.make_async_remote_copy(
            src_ref=pb.at[t, 8], dst_ref=pb.at[t, 0], send_sem=psend.at[t], recv_sem=precv.at[t],
            device_id=after, device_id_type=MESH,
        )

    def layer_copy(k):
        return pltpu.make_async_remote_copy(
            src_ref=layer.at[k], dst_ref=layer.at[3 + k], send_sem=qsend.at[k], recv_sem=qrecv.at[k],
            device_id=after, device_id_type=MESH,
        )

    def h_copy(j):
        at = pl.ds(4 * j, 4)
        return pltpu.make_async_remote_copy(
            src_ref=sent.at[:, at], dst_ref=got.at[:, at], send_sem=hsend.at[j], recv_sem=hrecv.at[j],
            device_id=other_event, device_id_type=MESH,
        )

    def end_copies(j):
        at = pl.ds(4 * j, 4)
        return [
            pltpu.make_async_copy(
                nat_u.at[k, at, e], end_hbm.at[e, at, :, pl.ds(128 * k, 128)], out_sem.at[j, 4 * e + k]
            )
            for e in range(2)
            for k in range(4)
        ]

    def hessian_copies(j):
        at = pl.ds(4 * j, 4)
        return [
            pltpu.make_async_copy(
                sent.at[k, at], hessian_hbm.at[at, :, pl.ds(128 * k, 128)], out_sem.at[j, 8 + k]
            )
            for k in range(4)
        ]

    set_up(0)
    pl.semaphore_wait(barrier, 4)
    u_copy(0).start()
    g_copy().start()
    gz_copy(0).start()
    set_up(7)
    gz_copy(7).start()

    @pl.loop(0, 16)
    def _(k):
        g = [gx[28 + i, k] for i in range(4)]
        v = [u[28 + i, k] for i in range(4)]
        scaled = [g[i] * float(DN[i, 4]) for i in range(4)]
        layer[2, k] = sum(scaled[i] * float(DN[i, 4]) for i in range(4))
        layer[0, k] = sum(
            scaled[i] * sum(float(DN[i, m]) * v[m] for m in range(4)) for i in range(4)
        )
        layer[1, k] = sum(float(DN[4, m]) * v[m] for m in range(4))

    for k in range(3):
        layer_copy(k).start()

    @pl.loop(0, 6)
    def _(n):
        set_up(6 - n)
        gz_copy(6 - n).start()

    def next_coefs(j):
        @pl.loop(0, 16)
        def _(k):
            g = [gx[4 * j + i, k] for i in range(5)]
            scaled = [g[i] * float(DN[i, 4]) for i in range(5)]
            for m in range(4):
                kx[j, m, k] = sum(scaled[i] * float(DN[i, m]) for i in range(5))
            kdx[j + 1, k] = sum(scaled[i] * float(DN[i, 4]) for i in range(5))

    def partial_x(t, j):
        @pl.loop(0, 4)
        def _(q):
            for s in range(4):
                k = 4 * q + s
                pb[t, j + 1, k] = (
                    kx[j, 0, k] * u[4 * j, k] + kx[j, 1, k] * u[4 * j + 1, k]
                ) + (kx[j, 2, k] * u[4 * j + 2, k] + kx[j, 3, k] * u[4 * j + 3, k])

    @pl.loop(0, 7)
    def _(j):
        next_coefs(j)
        partial_x(0, j)

    def send_z(t, j):
        @pl.when(slab == 0)
        def _():
            @pl.loop(0, 4)
            def _(xm):
                x = 4 * j + xm
                packed = [pack([u[x, 4 * zm + ym] for ym in range(4)], 3) for zm in range(4)]
                zs[t, x] = (kz[x, 0] * packed[0] + kz[x, 1] * packed[1]) + (
                    kz[x, 2] * packed[2] + kz[x, 3] * packed[3]
                )

        @pl.when(slab != 0)
        def _():
            for xm in range(4):
                x = 4 * j + xm
                zs[t, x] = pack([u[x, ym] for ym in range(4)], 0)

        z_copy(t, j).start()

    @pl.loop(0, 8)
    def _(n):
        j = lax.rem(7 * n, 8)
        gz_copy(j).wait_recv()

        @pl.loop(0, 4)
        def _(xm):
            x = 4 * j + xm
            arrived = gzh[x]
            above, below = arrived * is0, arrived * is1
            for ym in range(4):
                own = gz[x, ym]
                gz4[x, ym] = jnp.where(radial == 3, turn(above, 3 - ym), turn(own, 7))
                diagonal = turn(below, -ym) + is1 * float(DN[4, 4] ** 2) * own
                kdz[x, ym] = jnp.where(radial == 0, diagonal, 0.0)
            ends = [kz[x, zm] for zm in range(4)] + [arrived]
            scaled = [ends[i] * float(DN[i, 4]) for i in range(5)]
            for m in range(4):
                kz[x, m] = sum(scaled[i] * float(DN[i, m]) for i in range(5))

        send_z(0, j)

    def task(j, t):
        z_copy(t - 1, j).wait_recv()

        @pl.when(j == 0)
        def _():
            @pl.when(t > 1)
            def _():
                p_copy(t - 1).wait_recv()

        @pl.when(j == 7)
        def _():
            u_copy(t - 1).wait_recv()

        @pl.loop(0, 4)
        def _(xm):
            x = 4 * j + xm
            v = [[u[x, 4 * zm + ym] for ym in range(4)] for zm in range(4)]
            f = [[None] * 4 for _ in range(4)]
            arrived = zh[t - 1, x]
            above, below = arrived * is0, arrived * is1
            for ym in range(4):
                u4 = jnp.where(radial == 3, turn(above, 3 - ym), turn(v[0][ym], 7))
                parts = line(
                    *[v[zm][ym] for zm in range(4)], u4,
                    *[gz[x, 4 * zm + ym] for zm in range(4)], gz4[x, ym],
                )
                carried = jnp.where(radial == 0, turn(below, -ym), turn(parts[4], 1))
                f[0][ym] = (parts[0] + carried) + kdz[x, ym] * v[0][ym]
                f[1][ym], f[3][ym] = parts[1], parts[3]
                f[2][ym] = -parts[2]
            for zm in range(4):
                u4 = jnp.where(lane == 127, 0.0, pltpu.roll(v[zm][0], 127, 1))
                parts = line(
                    *v[zm], u4, *[gy[x, 4 * zm + ym] for ym in range(4)], gy4[x, zm]
                )
                carried = jnp.where(lane == 0, 0.0, pltpu.roll(parts[4], 1, 1))
                fs[xm, 4 * zm] = f[zm][0] + (parts[0] + carried)
                fs[xm, 4 * zm + 1] = f[zm][1] + parts[1]
                fs[xm, 4 * zm + 2] = f[zm][2] - parts[2]
                fs[xm, 4 * zm + 3] = f[zm][3] + parts[3]

        strength = jnp.where(upper, time_ref[0, t - 1], time_ref[1, t - 1])
        x = 4 * j

        @pl.loop(0, 4)
        def _(q):
            for s in range(4):
                k = 4 * q + s
                v = [u[x + i, k] for i in range(4)]
                parts = line(
                    *v, ub[t - 1, j + 1, k], *[gx[x + i, k] for i in range(5)], last=False
                )
                f = [
                    fs[0, k] + (parts[0] + (pb[t - 1, j, k] + kdx[j, k] * v[0])),
                    fs[1, k] + parts[1],
                    fs[2, k] - parts[2],
                    fs[3, k] + parts[3],
                ]
                for i in range(4):
                    kick = strength * sf[x + i, k] - im[x + i, k] * f[i]
                    speed = w[x + i, k] + kick
                    w[x + i, k] = speed
                    u[x + i, k] = v[i] + speed
                    hs[x + i, k] = hs[x + i, k] + kick * kick

        @pl.when(t < STEPS)
        def _():
            send_z(t, j)

            @pl.loop(0, 4)
            def _(q):
                for s in range(4):
                    ub[t, j, 4 * q + s] = u[x, 4 * q + s]

            partial_x(t, j)

            @pl.when(j == 0)
            def _():
                u_copy(t).start()

            @pl.when(j == 7)
            def _():
                p_copy(t).start()

        @pl.when(t == STEPS)
        def _():
            @pl.loop(0, 4)
            def _(zm):
                for half in range(2):
                    both = []
                    for ym in range(4):
                        one = hs[x + 2 * half, 4 * zm + ym]
                        two = hs[x + 2 * half + 1, 4 * zm + ym]
                        one = one + pltpu.roll(one, 4, 0)
                        two = two + pltpu.roll(two, 4, 0)
                        both.append(jnp.where(upper, one, two) * (100.0 / (4 * STEPS)))
                    for k, value in enumerate(together(both)):
                        rows_sent[pl.ds(512 * k + 16 * (x + 2 * half) + zm, 8, stride=4), :] = value

            h_copy(j).start()

            @pl.loop(0, 4)
            def _(zm):
                for xm in range(4):
                    whole = together([u[x + xm, 4 * zm + ym] for ym in range(4)])
                    for k, value in enumerate(whole):
                        rows_u[pl.ds(1024 * k + 32 * (x + xm) + zm, 8, stride=4), :] = value

            for copy in end_copies(j):
                copy.start()

    @pl.loop(1, 4)
    def _(t):
        @pl.loop(t, 8 - t)
        def _(j):
            task(j, t)

    g_copy().wait_recv()
    next_coefs(7)
    for k in range(3):
        layer_copy(k).wait_recv()

    @pl.loop(0, 16)
    def _(k):
        own = gx[0, k] * float(DN[4, 4])
        pb[0, 0, k] = layer[3, k] + own * layer[4, k]
        kdx[0, k] = layer[5, k] + own * float(DN[4, 4])

    @pl.loop(1, 5)
    def _(r):
        @pl.loop(0, 2 * (5 - r))
        def _(n):
            s = n // 2
            task(s + lax.rem(n, 2) * (7 - 2 * s), r + s)

    @pl.loop(0, 8)
    def _(n):
        s = n // 2
        j = 3 - s + lax.rem(n, 2) * (1 + 2 * s)
        h_copy(j).wait_recv()
        h_copy(j).wait_send()

        @pl.loop(0, 4)
        def _(xm):
            x = 4 * j + xm
            for k in range(4):
                sent[k, x] = sent[k, x] + got[k, x]

        for copy in hessian_copies(j):
            copy.start()

    u_copy(0).wait_send()
    g_copy().wait_send()
    for k in range(3):
        layer_copy(k).wait_send()
    for t in range(1, 4):
        u_copy(t).wait_send()
        p_copy(t).wait_send()

    @pl.loop(0, 8)
    def _(j):
        gz_copy(j).wait_send()
        for t in range(4):
            z_copy(t, j).wait_send()
        for copy in end_copies(j) + hessian_copies(j):
            copy.wait()


def per_device(slabs, blocks, *arrays):
    anywhere = pl.BlockSpec(memory_space=pl.ANY)
    field = pltpu.VMEM((32, 16, 8, 128), jnp.float32)
    scratch = [
        pltpu.VMEM((4, 32, 2, 16, 128), jnp.float32),
        pltpu.VMEM((4, 32, 2, 16, 128), jnp.float32),
        pltpu.VMEM((4, 32, 2, 16, 128), jnp.float32),
        pltpu.VMEM((4, 32, 16, 128), jnp.float32),
        pltpu.VMEM((4, 32, 16, 128), jnp.float32),
        pltpu.VMEM((32, 512), jnp.int32),
        field, field, field, field, field,
        pltpu.VMEM((33, 16, 8, 128), jnp.float32),
        field, field,
        pltpu.VMEM((32, 4, 8, 128), jnp.float32),
        pltpu.VMEM((32, 4, 8, 128), jnp.float32),
        pltpu.VMEM((8, 4, 16, 8, 128), jnp.float32),
        pltpu.VMEM((9, 16, 8, 128), jnp.float32),
        pltpu.VMEM((32, 4, 8, 128), jnp.float32),
        pltpu.VMEM((32, 4, 8, 128), jnp.float32),
        pltpu.VMEM((4, 9, 16, 8, 128), jnp.float32),
        pltpu.VMEM((4, 9, 16, 8, 128), jnp.float32),
        pltpu.VMEM((4, 16, 8, 128), jnp.float32),
        pltpu.VMEM((4, 32, 8, 128), jnp.float32),
        pltpu.VMEM((4, 32, 8, 128), jnp.float32),
        pltpu.VMEM((32, 8, 128), jnp.float32),
        pltpu.VMEM((32, 8, 128), jnp.float32),
        pltpu.VMEM((6, 16, 8, 128), jnp.float32),
        pltpu.VMEM((4, 32, 128), jnp.int32),
        pltpu.VMEM((4, 32, 16, 128), jnp.float32),
        pltpu.VMEM((4, 32, 16, 128), jnp.float32),
        pltpu.VMEM((8, 8, 128), jnp.int32),
        pltpu.SemaphoreType.DMA((9, 32)),
        pltpu.SemaphoreType.DMA((8, 12)),
        pltpu.SemaphoreType.DMA((5, 8)),
        pltpu.SemaphoreType.DMA((5, 8)),
        pltpu.SemaphoreType.DMA((5,)),
        pltpu.SemaphoreType.DMA((5,)),
        pltpu.SemaphoreType.DMA((4,)),
        pltpu.SemaphoreType.DMA((4,)),
        pltpu.SemaphoreType.DMA((3,)),
        pltpu.SemaphoreType.DMA((3,)),
        pltpu.SemaphoreType.DMA((8,)),
        pltpu.SemaphoreType.DMA((8,)),
    ]
    return pl.pallas_call(
        functools.partial(body, slabs, blocks),
        out_shape=(
            jax.ShapeDtypeStruct((2, 32, 16, 512), jnp.float32),
            jax.ShapeDtypeStruct((32, 16, 512), jnp.float32),
        ),
        in_specs=[anywhere] * 3 + [pl.BlockSpec(memory_space=pltpu.SMEM)] + [anywhere] * 3,
        out_specs=(anywhere, anywhere),
        scratch_shapes=scratch,
        compiler_params=pltpu.CompilerParams(
            collective_id=0, has_side_effects=True, vmem_limit_bytes=56 << 20
        ),
        name="adjoint_steps",
    )(*arrays)


def solution(mesh):
    in_specs = (
        P("event", "block", "slab", None),
        P("event", "block", "slab", None),
        P("event", "block", "slab", None),
        P("event", None),
        P("block", "slab", None),
        P("block", "slab", None),
        P("block", None),
    )
    out_specs = (P("event", "block", "slab", None), P("block", "slab", None))
    return jax.shard_map(
        functools.partial(per_device, mesh.shape["slab"], mesh.shape["block"]),
        mesh=mesh, in_specs=in_specs, out_specs=out_specs, check_vma=False,
    )
```

```python
import functools

import jax
import jax.numpy as jnp
import numpy as np
from jax import lax
from jax.experimental import pallas as pl
from jax.experimental.pallas import tpu as pltpu
from jax.sharding import PartitionSpec as P

STEPS = 4
TIME_STEP = 0.1
CRUST_FACTOR = 0.35
WEIGHTS = (0.1, 49.0 / 90.0, 32.0 / 45.0, 49.0 / 90.0, 0.1)
ASSEMBLED = (0.2, 49.0 / 90.0, 32.0 / 45.0, 49.0 / 90.0)
MESH = pl.DeviceIdType.MESH
TILE = (8, 128)


def derivative_table():
    points = np.array([-1.0, -np.sqrt(3.0 / 7.0), 0.0, np.sqrt(3.0 / 7.0), 1.0])
    scales = np.array(
        [
            np.prod([points[one] - points[other] for other in range(5) if other != one])
            for one in range(5)
        ]
    )
    table = np.zeros((5, 5))
    for target in range(5):
        for anchor in range(5):
            if target != anchor:
                table[target, anchor] = scales[target] / (
                    scales[anchor] * (points[target] - points[anchor])
                )
        table[target, target] = -np.sum(table[target])
    return table


D = derivative_table()
A4, B4 = (D[4, 4] - D[4, 0]) / 2, (D[4, 3] - D[4, 1]) / 2
E4, T4 = (D[4, 4] + D[4, 0]) / 2, (D[4, 3] + D[4, 1]) / 2
A3, B3 = (D[3, 4] - D[3, 0]) / 2, (D[3, 3] - D[3, 1]) / 2
E3, T3 = (D[3, 4] + D[3, 0]) / 2, (D[3, 3] + D[3, 1]) / 2
SCALE = (A4, A3, D[2, 3], A3, A4)
DN = D / np.array(SCALE)[:, None]
KAPPA0, GAMMA, DELTA = B4 / A4, E4 / A4, T4 / A4
KAPPA1, EPSILON, ZETA = B3 / A3, E3 / A3, T3 / A3
KAPPA2 = D[2, 4] / D[2, 3]
RHO = [WEIGHTS[i] * SCALE[i] ** 2 for i in range(5)]


def line(u0, u1, u2, u3, u4, c0, c1, c2, c3, c4, last=True):
    a, b = u4 - u0, u3 - u1
    twice = u2 + u2
    e, f = (u4 + u0) - twice, (u3 + u1) - twice
    p, q = a + KAPPA0 * b, GAMMA * e + DELTA * f
    r, s = a + KAPPA1 * b, EPSILON * e + ZETA * f
    h4, h0 = (p + q) * c4, (p - q) * c0
    h3, h1 = (r + s) * c3, (r - s) * c1
    h2 = (b + KAPPA2 * a) * c2
    hp, hm = h4 + h0, h4 - h0
    ep, em = h3 + h1, h3 - h1
    fa = (hp + ep) + KAPPA2 * h2
    fb = (KAPPA0 * hp + KAPPA1 * ep) + h2
    fe = GAMMA * hm + EPSILON * em
    ff = DELTA * hm + ZETA * em
    total = fe + ff
    return fe - fa, ff - fb, total + total, ff + fb, (fe + fa if last else None)


def body(slabs, blocks, *refs):
    (
        start_hbm, velocity_hbm, source_hbm, time_ref, modulus_hbm, mass_hbm, crust_hbm,
        end_ref, hessian_ref,
        nat_u, nat_v, nat_s, nat_g, nat_m, nat_c,
        u, w, sf, im, hs, gx, gy, gz, uy, gy4, gz4, kx, kdx, kz, kdz, ub, pb, fs, fy,
        zs, zh, gzs, gzh, layer, crust, sent, got, index,
        in_sem, end_sem, zsend, zrecv, gzsend, gzrecv, gsend, grecv,
        usend, urecv, psend, precv, qsend, qrecv, hsend, hrecv,
    ) = refs
    block = lax.axis_index("block")
    slab = lax.axis_index("slab")
    event = lax.axis_index("event")
    before = (lax.rem(block + blocks - 1, blocks), slab, event)
    after = (lax.rem(block + 1, blocks), slab, event)
    other_slab = (block, 1 - slab, event)
    other_event = (block, slab, 1 - event)

    barrier = pltpu.get_barrier_semaphore()
    for device in (before, after, other_slab, other_event):
        pl.semaphore_signal(barrier, inc=1, device_id=device, device_id_type=MESH)

    def start_loads(j):
        at = pl.ds(4 * j, 4)
        for k in range(4):
            lanes = (slice(None), pl.ds(128 * k, 128))
            pairs = [(modulus_hbm.at[at, *lanes], nat_g.at[k, at], 0)]
            for e in range(2):
                pairs.append((start_hbm.at[e, at, *lanes], nat_u.at[k, at, e], 1))
            pairs.append((mass_hbm.at[at, *lanes], nat_m.at[k, at], 2))
            for e in range(2):
                pairs.append((source_hbm.at[e, at, *lanes], nat_s.at[k, at, e], 3))
                pairs.append((velocity_hbm.at[e, at, *lanes], nat_v.at[k, at, e], 4))
            for source, target, kind in pairs:
                pltpu.make_async_copy(source, target, in_sem.at[j, kind]).start()

    def wait_load(ref, j, kind):
        whole = ref.at[:, pl.ds(4 * j, 4)]
        pltpu.make_async_copy(whole, whole, in_sem.at[j, kind]).wait()

    crust_load = pltpu.make_async_copy(crust_hbm, nat_c, gsend)
    crust_load.start()

    @pl.loop(0, 8)
    def _(n):
        start_loads(lax.rem(7 * n, 8))

    lane = lax.broadcasted_iota(jnp.int32, TILE, 1)
    row = lax.broadcasted_iota(jnp.int32, TILE, 0)
    radial = row & 3
    for r in range(4):
        index[r] = 4 * (lane & 31) + ((r - (lane >> 5)) & 3)
        index[4 + r] = 32 * ((r - (lane & 3)) & 3) + (lane >> 2)
    bit0, bit1 = (lane & 1) == 1, (lane & 2) == 2
    block0, block1 = (lane & 32) == 32, (lane & 64) == 64
    upper = row < 4
    is0 = jnp.where(slab == 0, 1.0, 0.0).astype(jnp.float32)
    is1 = 1.0 - is0

    def gather(value, k):
        return jnp.take_along_axis(value, index[k], axis=1)

    def apart(t):
        x = [jnp.where(bit0, t[(r + 3) % 4], t[r]) for r in range(4)]
        m = [jnp.where(bit1, x[(r + 2) % 4], x[r]) for r in range(4)]
        n = [gather(m[r], r) for r in range(4)]
        y = [jnp.where(block0, n[(k + 1) % 4], n[k]) for k in range(4)]
        return [jnp.where(block1, y[(k + 2) % 4], y[k]) for k in range(4)]

    def together(o):
        y = [jnp.where(block0, o[(r + 3) % 4], o[r]) for r in range(4)]
        n = [jnp.where(block1, y[(r + 2) % 4], y[r]) for r in range(4)]
        m = [gather(n[r], 4 + r) for r in range(4)]
        z = [jnp.where(bit0, m[(k + 1) % 4], m[k]) for k in range(4)]
        return [jnp.where(bit1, z[(k + 2) % 4], z[k]) for k in range(4)]

    def turn(value, shift):
        return value if shift % 8 == 0 else pltpu.roll(value, shift % 8, 0)

    def pack(values, at):
        result = turn(values[0], -at)
        for k in range(1, 4):
            result = jnp.where(radial == k, turn(values[k], k - at), result)
        return result

    def next_lane(value):
        return jnp.where(lane == 127, 0.0, pltpu.roll(value, 127, 1))

    def lane_before(value):
        return jnp.where(lane == 0, 0.0, pltpu.roll(value, 1, 1))

    def twice_events(value):
        other = pltpu.roll(value, 4, 0)
        return jnp.where(upper, value, other), jnp.where(upper, other, value)

    def rows_of(ref, per):
        return ref.reshape(4 * 32 * per, 128)

    rows_u, rows_v, rows_s = rows_of(nat_u, 32), rows_of(nat_v, 32), rows_of(nat_s, 32)
    rows_g, rows_m, rows_sent = rows_of(nat_g, 16), rows_of(nat_m, 16), rows_of(sent, 16)

    def strided(ref, first, count):
        return [ref[pl.ds(first + count * k, 8, stride=4), :] for k in range(4)]

    edge_z = jnp.where(slab == 0, jnp.where(radial == 0, 0.1, 0.2), 0.2).astype(jnp.float32)
    edge_y = jnp.where(lane == 0, 0.1, 0.2).astype(jnp.float32)

    def over_z(value, zm):
        return value * (edge_z if zm == 0 else ASSEMBLED[zm])

    def over_y(value, ym):
        return value * (edge_y if ym == 0 else ASSEMBLED[ym])

    crust_load.wait()

    @pl.loop(0, 4)
    def _(part):
        at = pl.ds(pl.multiple_of(8 * part, 8), 8)
        found = apart([nat_c[at, pl.ds(128 * k, 128)] for k in range(4)])
        for k in range(4):
            crust[k, at, :] = found[k]

    def set_up(j):
        wait_load(nat_g, j, 0)
        gxj, gyj, gzj = gx.at[j], gy.at[j], gz.at[j]
        for half in range(2):
            x = 4 * j + 2 * half
            depth = [
                jnp.where(
                    upper,
                    jnp.broadcast_to(crust[ym, pl.ds(x, 1), :], TILE),
                    jnp.broadcast_to(crust[ym, pl.ds(x + 1, 1), :], TILE),
                )
                for ym in range(4)
            ]
            for zm in range(4):
                moduli = apart(strided(rows_g, 16 * x + zm, 512))
                place = slab * 16 + 4 * radial + zm
                for ym in range(4):
                    stiff = jnp.where(
                        place >= 16 * slabs - depth[ym], CRUST_FACTOR * moduli[ym], moduli[ym]
                    )
                    at = 4 * zm + ym
                    for side, value in enumerate(twice_events(stiff)):
                        xm = 2 * half + side
                        in_y, in_z = over_y(value, ym), over_z(value, zm)
                        gxj[xm, at] = over_z(in_y, zm) * RHO[xm]
                        gyj[xm, at] = in_z * (RHO[ym] * ASSEMBLED[xm])
                        gzj[xm, at] = in_y * (RHO[zm] * ASSEMBLED[xm])
        for xm in range(4):
            for zm in range(4):
                gy4[j, xm, zm] = next_lane(gyj[xm, 4 * zm])
        wait_load(nat_u, j, 1)
        uj, ubj, uyj = u.at[j], ub.at[0, j], uy.at[j]
        for xm in range(4):
            x = 4 * j + xm
            for zm in range(4):
                values = apart(strided(rows_u, 32 * x + zm, 1024))
                for ym in range(4):
                    uj[xm, 4 * zm + ym] = values[ym]
                    if xm == 0:
                        ubj[4 * zm + ym] = values[ym]
                uyj[xm, zm] = next_lane(values[0])
        for xm in range(4):
            first = pack([gzj[xm, ym] for ym in range(4)], 0)
            ends = [pack([gzj[xm, 4 * zm + ym] for ym in range(4)], 3) for zm in range(4)]
            for zm in range(4):
                kz[j, xm, zm] = ends[zm]
            total = sum(ends[zm] * float(DN[zm, 4] ** 2) for zm in range(4))
            gzs[j, xm] = is0 * total + is1 * first

    def gz_copy(j, count=1):
        at = pl.ds(j, count)
        return pltpu.make_async_remote_copy(
            src_ref=gzs.at[at], dst_ref=gzh.at[at], send_sem=gzsend, recv_sem=gzrecv,
            device_id=other_slab, device_id_type=MESH,
        )

    def z_copy(t, j):
        return pltpu.make_async_remote_copy(
            src_ref=zs.at[t, j], dst_ref=zh.at[t, j], send_sem=zsend, recv_sem=zrecv.at[t, j],
            device_id=other_slab, device_id_type=MESH,
        )

    def u_copy(t):
        return pltpu.make_async_remote_copy(
            src_ref=ub.at[t, 0], dst_ref=ub.at[t, 8], send_sem=usend.at[t], recv_sem=urecv.at[t],
            device_id=before, device_id_type=MESH,
        )

    def g_copy():
        return pltpu.make_async_remote_copy(
            src_ref=gx.at[0, 0], dst_ref=gx.at[8, 0], send_sem=gsend, recv_sem=grecv,
            device_id=before, device_id_type=MESH,
        )

    def p_copy(t):
        return pltpu.make_async_remote_copy(
            src_ref=pb.at[t, 8], dst_ref=pb.at[t, 0], send_sem=psend.at[t], recv_sem=precv.at[t],
            device_id=after, device_id_type=MESH,
        )

    def layer_copy():
        return pltpu.make_async_remote_copy(
            src_ref=layer.at[pl.ds(0, 3)], dst_ref=layer.at[pl.ds(3, 3)], send_sem=qsend, recv_sem=qrecv,
            device_id=after, device_id_type=MESH,
        )

    def h_copy(j):
        at = pl.ds(4 * j, 4)
        return pltpu.make_async_remote_copy(
            src_ref=sent.at[:, at], dst_ref=got.at[:, at], send_sem=hsend.at[j], recv_sem=hrecv.at[j],
            device_id=other_event, device_id_type=MESH,
        )

    @pl.loop(0, 8)
    def _(n):
        j = lax.rem(7 * n, 8)
        set_up(j)

        @pl.when(n == 0)
        def _():
            pl.semaphore_wait(barrier, 4)
            u_copy(0).start()
            g_copy().start()

        gz_copy(j).start()

        @pl.when(n == 1)
        def _():
            for k in range(16):
                g = [gx[7, i, k] for i in range(4)]
                v = [u[7, i, k] for i in range(4)]
                scaled = [g[i] * float(DN[i, 4]) for i in range(4)]
                layer[2, k] = sum(scaled[i] * float(DN[i, 4]) for i in range(4))
                layer[0, k] = sum(
                    scaled[i] * sum(float(DN[i, m]) * v[m] for m in range(4)) for i in range(4)
                )
                layer[1, k] = sum(float(DN[4, m]) * v[m] for m in range(4))
            layer_copy().start()

    def next_coefs(j):
        gj, gn, kj, kn = gx.at[j], gx.at[j + 1, 0], kx.at[j], kdx.at[j + 1]
        for k in range(16):
            scaled = [gj[i, k] * float(DN[i, 4]) for i in range(4)] + [gn[k] * float(DN[4, 4])]
            for m in range(4):
                kj[m, k] = sum(scaled[i] * float(DN[i, m]) for i in range(5))
            kn[k] = sum(scaled[i] * float(DN[i, 4]) for i in range(5))

    def partial_x(t, j):
        uj, kj, pj = u.at[j], kx.at[j], pb.at[t, j + 1]
        for k in range(16):
            pj[k] = (kj[0, k] * uj[0, k] + kj[1, k] * uj[1, k]) + (
                kj[2, k] * uj[2, k] + kj[3, k] * uj[3, k]
            )

    @pl.loop(0, 7)
    def _(j):
        next_coefs(j)
        partial_x(0, j)

    def send_z(t, j):
        uj, zj = u.at[j], zs.at[t, j]

        @pl.when(slab == 0)
        def _():
            kj = kz.at[j]
            for xm in range(4):
                packed = [pack([uj[xm, 4 * zm + ym] for ym in range(4)], 3) for zm in range(4)]
                zj[xm] = (kj[xm, 0] * packed[0] + kj[xm, 1] * packed[1]) + (
                    kj[xm, 2] * packed[2] + kj[xm, 3] * packed[3]
                )

        @pl.when(slab != 0)
        def _():
            for xm in range(4):
                zj[xm] = pack([uj[xm, ym] for ym in range(4)], 0)

        z_copy(t, j).start()

    gz_copy(0, 8).wait_recv()

    @pl.loop(0, 8)
    def _(n):
        j = lax.rem(n + 1, 8)
        gzj, gz4j, kzj, kdzj, gzhj = gz.at[j], gz4.at[j], kz.at[j], kdz.at[j], gzh.at[j]
        for xm in range(4):
            arrived = gzhj[xm]
            above, below = arrived * is0, arrived * is1
            for ym in range(4):
                own = gzj[xm, ym]
                gz4j[xm, ym] = jnp.where(radial == 3, turn(above, 3 - ym), turn(own, 7))
                diagonal = turn(below, -ym) + is1 * float(DN[4, 4] ** 2) * own
                kdzj[xm, ym] = jnp.where(radial == 0, diagonal, 0.0)
            ends = [kzj[xm, zm] for zm in range(4)] + [arrived]
            scaled = [ends[i] * float(DN[i, 4]) for i in range(5)]
            for m in range(4):
                kzj[xm, m] = sum(scaled[i] * float(DN[i, m]) for i in range(5))
        send_z(0, j)

    def advance(j, t, first):
        z_copy(t - 1, j).wait_recv()
        uj, gxj, gyj, gzj, uyj = u.at[j], gx.at[j], gy.at[j], gz.at[j], uy.at[j]
        gy4j, gz4j, kdzj, zhj = gy4.at[j], gz4.at[j], kdz.at[j], zh.at[t - 1, j]
        imj, sfj, wj, hsj = im.at[j], sf.at[j], w.at[j], hs.at[j]
        if first:
            wait_load(nat_m, j, 2)
            wait_load(nat_s, j, 3)
            wait_load(nat_v, j, 4)

        for xm in range(4):
            x = 4 * j + xm
            if first:
                for zm in range(4):
                    if xm % 2 == 0:
                        masses = apart(strided(rows_m, 16 * x + zm, 512))
                        for ym in range(4):
                            mass = masses[ym] * (TIME_STEP * TIME_STEP)
                            one, two = twice_events(mass)
                            imj[xm, 4 * zm + ym], imj[xm + 1, 4 * zm + ym] = one, two
                    values = apart(strided(rows_v, 32 * x + zm, 1024))
                    for ym in range(4):
                        wj[xm, 4 * zm + ym] = values[ym] * TIME_STEP
                    values = apart(strided(rows_s, 32 * x + zm, 1024))
                    for ym in range(4):
                        sfj[xm, 4 * zm + ym] = values[ym] * imj[xm, 4 * zm + ym]
            v = [[uj[xm, 4 * zm + ym] for ym in range(4)] for zm in range(4)]
            f = [[None] * 4 for _ in range(4)]
            arrived = zhj[xm]
            above, below = arrived * is0, arrived * is1
            for ym in range(4):
                u4 = jnp.where(radial == 3, turn(above, 3 - ym), turn(v[0][ym], 7))
                parts = line(
                    *[v[zm][ym] for zm in range(4)], u4,
                    *[gzj[xm, 4 * zm + ym] for zm in range(4)], gz4j[xm, ym],
                )
                carried = jnp.where(radial == 0, turn(below, -ym), turn(parts[4], 1))
                f[0][ym] = (parts[0] + carried) + kdzj[xm, ym] * v[0][ym]
                f[1][ym], f[3][ym] = parts[1], parts[3]
                f[2][ym] = -parts[2]
            for zm in range(4):
                parts = line(
                    *v[zm], uyj[xm, zm], *[gyj[xm, 4 * zm + ym] for ym in range(4)], gy4j[xm, zm]
                )
                fy[xm, zm] = lane_before(parts[4])
                fs[xm, 4 * zm] = f[zm][0] + parts[0]
                fs[xm, 4 * zm + 1] = f[zm][1] + parts[1]
                fs[xm, 4 * zm + 2] = f[zm][2] - parts[2]
                fs[xm, 4 * zm + 3] = f[zm][3] + parts[3]

        strength = jnp.where(upper, time_ref[0, t - 1], time_ref[1, t - 1])
        ubn, pbj, kdxj, gxn = ub.at[t - 1, j + 1], pb.at[t - 1, j], kdx.at[j], gx.at[j + 1, 0]
        for k in range(16):
            v = [uj[i, k] for i in range(4)]
            parts = line(*v, ubn[k], *[gxj[i, k] for i in range(4)], gxn[k], last=False)
            f = [
                fs[0, k] + (parts[0] + (pbj[k] + kdxj[k] * v[0])),
                fs[1, k] + parts[1],
                fs[2, k] - parts[2],
                fs[3, k] + parts[3],
            ]
            for i in range(4):
                if k % 4 == 0:
                    f[i] = f[i] + fy[i, k // 4]
                kick = strength * sfj[i, k] - imj[i, k] * f[i]
                speed = wj[i, k] + kick
                wj[i, k] = speed
                moved = v[i] + speed
                uj[i, k] = moved
                hsj[i, k] = kick * kick if first else hsj[i, k] + kick * kick
                if k % 4 == 0:
                    uyj[i, k // 4] = next_lane(moved)

    def hand_on(j, t):
        send_z(t, j)
        uj, ubj = u.at[j], ub.at[t, j]
        for k in range(16):
            ubj[k] = uj[0, k]
        partial_x(t, j)

        @pl.when(j == 0)
        def _():
            u_copy(t).start()

        @pl.when(j == 7)
        def _():
            p_copy(t).start()

    def end_copy(j, k, e):
        at = pl.ds(4 * j, 4)
        return pltpu.make_async_copy(
            nat_u.at[k, at, e], end_ref.at[e, at, :, pl.ds(128 * k, 128)], end_sem
        )

    def finish(j):
        uj, hsj = u.at[j], hs.at[j]
        for half in range(2):
            for zm in range(4):
                both = []
                for ym in range(4):
                    one, two = hsj[2 * half, 4 * zm + ym], hsj[2 * half + 1, 4 * zm + ym]
                    one = one + pltpu.roll(one, 4, 0)
                    two = two + pltpu.roll(two, 4, 0)
                    both.append(jnp.where(upper, one, two) * (100.0 / (4 * STEPS)))
                for k, value in enumerate(together(both)):
                    first = 512 * k + 16 * (4 * j + 2 * half) + zm
                    rows_sent[pl.ds(first, 8, stride=4), :] = value
        h_copy(j).start()
        for xm in range(4):
            for zm in range(4):
                whole = together([uj[xm, 4 * zm + ym] for ym in range(4)])
                for k, value in enumerate(whole):
                    rows_u[pl.ds(1024 * k + 32 * (4 * j + xm) + zm, 8, stride=4), :] = value
        for k in range(4):
            for e in range(2):
                end_copy(j, k, e).start()

    @pl.loop(0, 8)
    def _(n):
        j = lax.rem(n + 1, 7) + 6 * (n // 7)

        @pl.when(n == 6)
        def _():
            layer_copy().wait_recv()
            for k in range(16):
                own = gx[0, 0, k] * float(DN[4, 4])
                pb[0, 0, k] = layer[3, k] + own * layer[4, k]
                kdx[0, k] = layer[5, k] + own * float(DN[4, 4])

        @pl.when(n == 7)
        def _():
            u_copy(0).wait_recv()
            g_copy().wait_recv()
            next_coefs(7)

        advance(j, 1, True)
        hand_on(j, 1)

    def digit(n, digits, bits):
        words = [
            sum(d << (bits * i) for i, d in enumerate(digits[s : s + 8])) for s in (0, 8, 16)
        ]
        word = jnp.where(n < 8, words[0], jnp.where(n < 16, words[1], words[2]))
        return (word >> (bits * (n & 7))) & ((1 << bits) - 1)

    order_j = (2, 3, 4, 5, 3, 4, 1, 6, 2, 5, 3, 4, 0, 7, 1, 6, 2, 5, 0, 7, 1, 6, 0, 7)
    order_t = (2, 2, 2, 2, 3, 3, 2, 2, 3, 3, 4, 4, 2, 2, 3, 3, 4, 4, 3, 3, 4, 4, 4, 4)

    @pl.loop(0, 24)
    def _(n):
        j = digit(n, order_j, 3)
        t = digit(n, order_t, 3)

        @pl.when(j == 0)
        def _():
            p_copy(t - 1).wait_recv()

        @pl.when(j == 7)
        def _():
            u_copy(t - 1).wait_recv()

        advance(j, t, False)

        @pl.when(t < STEPS)
        def _():
            hand_on(j, t)

        @pl.when(t == STEPS)
        def _():
            finish(j)

    @pl.loop(0, 8)
    def _(n):
        s = n // 2
        j = 3 - s + lax.rem(n, 2) * (1 + 2 * s)
        h_copy(j).wait_recv()
        for xm in range(4):
            x = 4 * j + xm
            for k in range(4):
                hessian_ref[x, :, pl.ds(128 * k, 128)] = sent[k, x] + got[k, x]

    u_copy(0).wait_send()
    g_copy().wait_send()
    layer_copy().wait_send()
    gz_copy(0, 8).wait_send()
    for t in range(1, 4):
        u_copy(t).wait_send()
        p_copy(t).wait_send()

    @pl.loop(0, 8)
    def _(j):
        h_copy(j).wait_send()

    pltpu.make_async_copy(zs, zs, zsend).wait()
    pltpu.make_async_copy(nat_u, nat_u, end_sem).wait()


def per_device(slabs, blocks, *arrays):
    anywhere = pl.BlockSpec(memory_space=pl.ANY)
    inside = pl.BlockSpec(memory_space=pltpu.VMEM)

    def tiles(*shape):
        return pltpu.VMEM((*shape, 8, 128), jnp.float32)

    field, natural = tiles(8, 4, 16), pltpu.VMEM((4, 32, 16, 128), jnp.float32)
    natural_events = pltpu.VMEM((4, 32, 2, 16, 128), jnp.float32)
    several = pltpu.SemaphoreType.DMA
    scratch = [
        natural_events, natural_events, natural_events,
        natural, natural, pltpu.VMEM((32, 512), jnp.int32),
        field, field, field, field, field,
        tiles(9, 4, 16), field, field,
        tiles(8, 4, 4), tiles(8, 4, 4), tiles(8, 4, 4),
        tiles(8, 4, 16), tiles(9, 16), tiles(8, 4, 4), tiles(8, 4, 4),
        tiles(4, 9, 16), tiles(4, 9, 16), tiles(4, 16), tiles(4, 4),
        tiles(4, 8, 4), tiles(4, 8, 4), tiles(8, 4), tiles(8, 4),
        tiles(6, 16), pltpu.VMEM((4, 32, 128), jnp.int32),
        natural, natural, pltpu.VMEM((8, 8, 128), jnp.int32),
        several((8, 5)), several, several, several((4, 8)),
        several, several, several, several,
        several((4,)), several((4,)), several((4,)), several((4,)),
        several, several, several((8,)), several((8,)),
    ]
    return pl.pallas_call(
        functools.partial(body, slabs, blocks),
        out_shape=(
            pltpu.VMEM((2, 32, 16, 512), jnp.float32),
            pltpu.VMEM((32, 16, 512), jnp.float32),
        ),
        in_specs=[anywhere] * 3 + [pl.BlockSpec(memory_space=pltpu.SMEM)] + [anywhere] * 3,
        out_specs=(inside, inside),
        scratch_shapes=scratch,
        compiler_params=pltpu.CompilerParams(
            collective_id=0, has_side_effects=True, vmem_limit_bytes=56 << 20
        ),
        name="adjoint_steps",
    )(*arrays)


def solution(mesh):
    in_specs = (
        P("event", "block", "slab", None),
        P("event", "block", "slab", None),
        P("event", "block", "slab", None),
        P("event", None),
        P("block", "slab", None),
        P("block", "slab", None),
        P("block", None),
    )
    out_specs = (P("event", "block", "slab", None), P("block", "slab", None))
    return jax.shard_map(
        functools.partial(per_device, mesh.shape["slab"], mesh.shape["block"]),
        mesh=mesh, in_specs=in_specs, out_specs=out_specs, check_vma=False,
    )
```

```python
import functools

import jax
import jax.numpy as jnp
import numpy as np
from jax import lax
from jax.experimental import pallas as pl
from jax.experimental.pallas import tpu as pltpu
from jax.sharding import PartitionSpec as P

STEPS = 4
TIME_STEP = 0.1
CRUST_FACTOR = 0.35
WEIGHTS = (0.1, 49.0 / 90.0, 32.0 / 45.0, 49.0 / 90.0, 0.1)
ASSEMBLED = (0.2, 49.0 / 90.0, 32.0 / 45.0, 49.0 / 90.0)
MESH = pl.DeviceIdType.MESH
TILE = (8, 128)


def derivative_table():
    points = np.array([-1.0, -np.sqrt(3.0 / 7.0), 0.0, np.sqrt(3.0 / 7.0), 1.0])
    scales = np.array(
        [
            np.prod([points[one] - points[other] for other in range(5) if other != one])
            for one in range(5)
        ]
    )
    table = np.zeros((5, 5))
    for target in range(5):
        for anchor in range(5):
            if target != anchor:
                table[target, anchor] = scales[target] / (
                    scales[anchor] * (points[target] - points[anchor])
                )
        table[target, target] = -np.sum(table[target])
    return table


D = derivative_table()
A4, B4 = (D[4, 4] - D[4, 0]) / 2, (D[4, 3] - D[4, 1]) / 2
E4, T4 = (D[4, 4] + D[4, 0]) / 2, (D[4, 3] + D[4, 1]) / 2
A3, B3 = (D[3, 4] - D[3, 0]) / 2, (D[3, 3] - D[3, 1]) / 2
E3, T3 = (D[3, 4] + D[3, 0]) / 2, (D[3, 3] + D[3, 1]) / 2
SCALE = (A4, A3, D[2, 3], A3, A4)
DN = D / np.array(SCALE)[:, None]
KAPPA0, GAMMA, DELTA = B4 / A4, E4 / A4, T4 / A4
KAPPA1, EPSILON, ZETA = B3 / A3, E3 / A3, T3 / A3
KAPPA2 = D[2, 4] / D[2, 3]
RHO = [WEIGHTS[i] * SCALE[i] ** 2 for i in range(5)]


def line(u0, u1, u2, u3, u4, c0, c1, c2, c3, c4, last=True):
    a, b = u4 - u0, u3 - u1
    twice = u2 + u2
    e, f = (u4 + u0) - twice, (u3 + u1) - twice
    p, q = a + KAPPA0 * b, GAMMA * e + DELTA * f
    r, s = a + KAPPA1 * b, EPSILON * e + ZETA * f
    h4, h0 = (p + q) * c4, (p - q) * c0
    h3, h1 = (r + s) * c3, (r - s) * c1
    h2 = (b + KAPPA2 * a) * c2
    hp, hm = h4 + h0, h4 - h0
    ep, em = h3 + h1, h3 - h1
    fa = (hp + ep) + KAPPA2 * h2
    fb = (KAPPA0 * hp + KAPPA1 * ep) + h2
    fe = GAMMA * hm + EPSILON * em
    ff = DELTA * hm + ZETA * em
    total = fe + ff
    return fe - fa, ff - fb, total + total, ff + fb, (fe + fa if last else None)


ORDER = (
    (4, 1), (3, 1), (2, 1), (1, 1), (7, 1), (2, 2), (0, 1), (6, 1), (5, 1), (3, 2), (4, 2), (1, 2),
    (2, 3), (0, 2), (1, 3), (7, 2), (3, 3), (2, 4), (5, 2), (6, 2), (4, 3), (3, 4), (6, 3), (0, 3),
    (5, 3), (1, 4), (7, 3), (5, 4), (4, 4), (6, 4), (0, 4), (7, 4),
)
FIRST_ORDER = [j for j, t in ORDER if t == 1]
LAST_ORDER = [j for j, t in ORDER if t == STEPS]


def digit(n, digits, bits):
    words = [
        sum(d << (bits * i) for i, d in enumerate(digits[s : s + 7])) for s in range(0, len(digits), 7)
    ]
    word, place = words[0], n
    for i in range(1, len(words)):
        word = jnp.where(n < 7 * i, word, words[i])
        place = jnp.where(n < 7 * i, place, n - 7 * i)
    return (word >> (bits * place)) & ((1 << bits) - 1)


def place_out(end_in, hessian_in, end_out, hessian_out, sem):
    pairs = [(end_in.at[e, pl.ds(16 * h, 16)], end_out.at[e, pl.ds(16 * h, 16)]) for e in range(2) for h in range(2)]
    pairs += [(hessian_in.at[pl.ds(16 * h, 16)], hessian_out.at[pl.ds(16 * h, 16)]) for h in range(2)]
    copies = [pltpu.make_async_copy(*pair, sem.at[i]) for i, pair in enumerate(pairs)]
    for copy in copies:
        copy.start()
    for copy in copies:
        copy.wait()


def body(slabs, blocks, *refs):
    (
        start_hbm, velocity_hbm, source_hbm, time_ref, modulus_hbm, mass_hbm, crust_hbm,
        end_ref, hessian_ref,
        nat_u, nat_v, nat_s, nat_g, nat_m, nat_c,
        u, w, sf, im, hs, gx, gy, gz, uy, gy4, gz4, kx, kdx, kz, kdz, ub, pb, fs, fy,
        zs, zh, gzs, gzh, layer, crust, sent, got, index,
        in_sem, end_sem, zsend, zrecv, gzsend, gzrecv, gsend, grecv,
        usend, urecv, psend, precv, qsend, qrecv, hsend, hrecv,
    ) = refs
    block = lax.axis_index("block")
    slab = lax.axis_index("slab")
    event = lax.axis_index("event")
    before = (lax.rem(block + blocks - 1, blocks), slab, event)
    after = (lax.rem(block + 1, blocks), slab, event)
    other_slab = (block, 1 - slab, event)
    other_event = (block, slab, 1 - event)

    barrier = pltpu.get_barrier_semaphore()
    for device in (before, after, other_slab, other_event):
        pl.semaphore_signal(barrier, inc=1, device_id=device, device_id_type=MESH)

    def start_loads(j, late):
        at = pl.ds(4 * j, 4)
        for k in range(4):
            lanes = (slice(None), pl.ds(128 * k, 128))
            if late:
                pairs = [(mass_hbm.at[at, *lanes], nat_m.at[k, at], 2)]
                for e in range(2):
                    pairs.append((source_hbm.at[e, at, *lanes], nat_s.at[k, at, e], 3))
                    pairs.append((velocity_hbm.at[e, at, *lanes], nat_v.at[k, at, e], 4))
            else:
                pairs = [(modulus_hbm.at[at, *lanes], nat_g.at[k, at], 0)]
                for e in range(2):
                    pairs.append((start_hbm.at[e, at, *lanes], nat_u.at[k, at, e], 1))
            for source, target, kind in pairs:
                pltpu.make_async_copy(source, target, in_sem.at[j, kind]).start()

    def wait_load(ref, j, kind):
        whole = ref.at[:, pl.ds(4 * j, 4)]
        pltpu.make_async_copy(whole, whole, in_sem.at[j, kind]).wait()

    crust_load = pltpu.make_async_copy(crust_hbm, nat_c, gsend)
    crust_load.start()

    @pl.loop(0, 8)
    def _(n):
        start_loads(lax.rem(7 * n, 8), False)

    @pl.loop(0, 8)
    def _(n):
        start_loads(digit(n, FIRST_ORDER, 4), True)

    lane = lax.broadcasted_iota(jnp.int32, TILE, 1)
    row = lax.broadcasted_iota(jnp.int32, TILE, 0)
    radial = row & 3
    for r in range(4):
        index[r] = 4 * (lane & 31) + ((r - (lane >> 5)) & 3)
        index[4 + r] = 32 * ((r - (lane & 3)) & 3) + (lane >> 2)
    bit0, bit1 = (lane & 1) == 1, (lane & 2) == 2
    block0, block1 = (lane & 32) == 32, (lane & 64) == 64
    upper = row < 4
    is0 = jnp.where(slab == 0, 1.0, 0.0).astype(jnp.float32)
    is1 = 1.0 - is0

    def gather(value, k):
        return jnp.take_along_axis(value, index[k], axis=1)

    def apart(t):
        x = [jnp.where(bit0, t[(r + 3) % 4], t[r]) for r in range(4)]
        m = [jnp.where(bit1, x[(r + 2) % 4], x[r]) for r in range(4)]
        n = [gather(m[r], r) for r in range(4)]
        y = [jnp.where(block0, n[(k + 1) % 4], n[k]) for k in range(4)]
        return [jnp.where(block1, y[(k + 2) % 4], y[k]) for k in range(4)]

    def together(o):
        y = [jnp.where(block0, o[(r + 3) % 4], o[r]) for r in range(4)]
        n = [jnp.where(block1, y[(r + 2) % 4], y[r]) for r in range(4)]
        m = [gather(n[r], 4 + r) for r in range(4)]
        z = [jnp.where(bit0, m[(k + 1) % 4], m[k]) for k in range(4)]
        return [jnp.where(bit1, z[(k + 2) % 4], z[k]) for k in range(4)]

    def turn(value, shift):
        return value if shift % 8 == 0 else pltpu.roll(value, shift % 8, 0)

    def pack(values, at):
        result = turn(values[0], -at)
        for k in range(1, 4):
            result = jnp.where(radial == k, turn(values[k], k - at), result)
        return result

    def next_lane(value):
        return jnp.where(lane == 127, 0.0, pltpu.roll(value, 127, 1))

    def lane_before(value):
        return jnp.where(lane == 0, 0.0, pltpu.roll(value, 1, 1))

    def twice_events(value):
        other = pltpu.roll(value, 4, 0)
        return jnp.where(upper, value, other), jnp.where(upper, other, value)

    def rows_of(ref, per):
        return ref.reshape(4 * 32 * per, 128)

    rows_u, rows_v, rows_s = rows_of(nat_u, 32), rows_of(nat_v, 32), rows_of(nat_s, 32)
    rows_g, rows_m, rows_sent = rows_of(nat_g, 16), rows_of(nat_m, 16), rows_of(sent, 16)

    def strided(ref, first, count):
        return [ref[pl.ds(first + count * k, 8, stride=4), :] for k in range(4)]

    edge_z = jnp.where(slab == 0, jnp.where(radial == 0, 0.1, 0.2), 0.2).astype(jnp.float32)
    edge_y = jnp.where(lane == 0, 0.1, 0.2).astype(jnp.float32)

    def over_z(value, zm):
        return value * (edge_z if zm == 0 else ASSEMBLED[zm])

    def over_y(value, ym):
        return value * (edge_y if ym == 0 else ASSEMBLED[ym])

    crust_load.wait()

    @pl.loop(0, 4)
    def _(part):
        at = pl.ds(pl.multiple_of(8 * part, 8), 8)
        found = apart([nat_c[at, pl.ds(128 * k, 128)] for k in range(4)])
        for k in range(4):
            crust[k, at, :] = found[k]

    def set_up(j):
        wait_load(nat_g, j, 0)
        gxj, gyj, gzj = gx.at[j], gy.at[j], gz.at[j]
        for half in range(2):
            x = 4 * j + 2 * half
            depth = [
                jnp.where(
                    upper,
                    jnp.broadcast_to(crust[ym, pl.ds(x, 1), :], TILE),
                    jnp.broadcast_to(crust[ym, pl.ds(x + 1, 1), :], TILE),
                )
                for ym in range(4)
            ]
            for zm in range(4):
                moduli = apart(strided(rows_g, 16 * x + zm, 512))
                place = slab * 16 + 4 * radial + zm
                for ym in range(4):
                    stiff = jnp.where(
                        place >= 16 * slabs - depth[ym], CRUST_FACTOR * moduli[ym], moduli[ym]
                    )
                    at = 4 * zm + ym
                    for side, value in enumerate(twice_events(stiff)):
                        xm = 2 * half + side
                        in_y, in_z = over_y(value, ym), over_z(value, zm)
                        gxj[xm, at] = over_z(in_y, zm) * RHO[xm]
                        gyj[xm, at] = in_z * (RHO[ym] * ASSEMBLED[xm])
                        gzj[xm, at] = in_y * (RHO[zm] * ASSEMBLED[xm])
        for xm in range(4):
            for zm in range(4):
                gy4[j, xm, zm] = next_lane(gyj[xm, 4 * zm])
        wait_load(nat_u, j, 1)
        uj, ubj, uyj = u.at[j], ub.at[0, j], uy.at[j]
        for xm in range(4):
            x = 4 * j + xm
            for zm in range(4):
                values = apart(strided(rows_u, 32 * x + zm, 1024))
                for ym in range(4):
                    uj[xm, 4 * zm + ym] = values[ym]
                    if xm == 0:
                        ubj[4 * zm + ym] = values[ym]
                uyj[xm, zm] = next_lane(values[0])
        for xm in range(4):
            first = pack([gzj[xm, ym] for ym in range(4)], 0)
            ends = [pack([gzj[xm, 4 * zm + ym] for ym in range(4)], 3) for zm in range(4)]
            for zm in range(4):
                kz[j, xm, zm] = ends[zm]
            total = sum(ends[zm] * float(DN[zm, 4] ** 2) for zm in range(4))
            gzs[j, xm] = is0 * total + is1 * first

    def gz_copy(j, count=1):
        at = pl.ds(j, count)
        return pltpu.make_async_remote_copy(
            src_ref=gzs.at[at], dst_ref=gzh.at[at], send_sem=gzsend, recv_sem=gzrecv,
            device_id=other_slab, device_id_type=MESH,
        )

    def z_copy(t, j):
        return pltpu.make_async_remote_copy(
            src_ref=zs.at[t, j], dst_ref=zh.at[t, j], send_sem=zsend, recv_sem=zrecv.at[t, j],
            device_id=other_slab, device_id_type=MESH,
        )

    def u_copy(t):
        return pltpu.make_async_remote_copy(
            src_ref=ub.at[t, 0], dst_ref=ub.at[t, 8], send_sem=usend.at[t], recv_sem=urecv.at[t],
            device_id=before, device_id_type=MESH,
        )

    def g_copy():
        return pltpu.make_async_remote_copy(
            src_ref=gx.at[0, 0], dst_ref=gx.at[8, 0], send_sem=gsend, recv_sem=grecv,
            device_id=before, device_id_type=MESH,
        )

    def p_copy(t):
        return pltpu.make_async_remote_copy(
            src_ref=pb.at[t, 8], dst_ref=pb.at[t, 0], send_sem=psend.at[t], recv_sem=precv.at[t],
            device_id=after, device_id_type=MESH,
        )

    def layer_copy():
        return pltpu.make_async_remote_copy(
            src_ref=layer.at[pl.ds(0, 3)], dst_ref=layer.at[pl.ds(3, 3)], send_sem=qsend, recv_sem=qrecv,
            device_id=after, device_id_type=MESH,
        )

    def h_copy(j):
        at = pl.ds(4 * j, 4)
        return pltpu.make_async_remote_copy(
            src_ref=sent.at[:, at], dst_ref=got.at[:, at], send_sem=hsend.at[j], recv_sem=hrecv.at[j],
            device_id=other_event, device_id_type=MESH,
        )

    @pl.loop(0, 8)
    def _(n):
        j = lax.rem(7 * n, 8)
        set_up(j)

        @pl.when(n == 0)
        def _():
            pl.semaphore_wait(barrier, 4)
            u_copy(0).start()
            g_copy().start()

        gz_copy(j).start()

        @pl.when(n == 1)
        def _():
            for k in range(16):
                g = [gx[7, i, k] for i in range(4)]
                v = [u[7, i, k] for i in range(4)]
                scaled = [g[i] * float(DN[i, 4]) for i in range(4)]
                layer[2, k] = sum(scaled[i] * float(DN[i, 4]) for i in range(4))
                layer[0, k] = sum(
                    scaled[i] * sum(float(DN[i, m]) * v[m] for m in range(4)) for i in range(4)
                )
                layer[1, k] = sum(float(DN[4, m]) * v[m] for m in range(4))
            layer_copy().start()

    def next_coefs(j):
        gj, gn, kj, kn = gx.at[j], gx.at[j + 1, 0], kx.at[j], kdx.at[j + 1]
        for k in range(16):
            scaled = [gj[i, k] * float(DN[i, 4]) for i in range(4)] + [gn[k] * float(DN[4, 4])]
            for m in range(4):
                kj[m, k] = sum(scaled[i] * float(DN[i, m]) for i in range(5))
            kn[k] = sum(scaled[i] * float(DN[i, 4]) for i in range(5))

    def partial_x(t, j):
        uj, kj, pj = u.at[j], kx.at[j], pb.at[t, j + 1]
        for k in range(16):
            pj[k] = (kj[0, k] * uj[0, k] + kj[1, k] * uj[1, k]) + (
                kj[2, k] * uj[2, k] + kj[3, k] * uj[3, k]
            )

    @pl.loop(0, 7)
    def _(j):
        next_coefs(j)
        partial_x(0, j)

    def send_z(t, j):
        uj, zj = u.at[j], zs.at[t, j]

        @pl.when(slab == 0)
        def _():
            kj = kz.at[j]
            for xm in range(4):
                packed = [pack([uj[xm, 4 * zm + ym] for ym in range(4)], 3) for zm in range(4)]
                zj[xm] = (kj[xm, 0] * packed[0] + kj[xm, 1] * packed[1]) + (
                    kj[xm, 2] * packed[2] + kj[xm, 3] * packed[3]
                )

        @pl.when(slab != 0)
        def _():
            for xm in range(4):
                zj[xm] = pack([uj[xm, ym] for ym in range(4)], 0)

        z_copy(t, j).start()

    gz_copy(0, 8).wait_recv()

    @pl.loop(0, 8)
    def _(n):
        j = lax.rem(n + 1, 8)
        gzj, gz4j, kzj, kdzj, gzhj = gz.at[j], gz4.at[j], kz.at[j], kdz.at[j], gzh.at[j]
        for xm in range(4):
            arrived = gzhj[xm]
            above, below = arrived * is0, arrived * is1
            for ym in range(4):
                own = gzj[xm, ym]
                gz4j[xm, ym] = jnp.where(radial == 3, turn(above, 3 - ym), turn(own, 7))
                diagonal = turn(below, -ym) + is1 * float(DN[4, 4] ** 2) * own
                kdzj[xm, ym] = jnp.where(radial == 0, diagonal, 0.0)
            ends = [kzj[xm, zm] for zm in range(4)] + [arrived]
            scaled = [ends[i] * float(DN[i, 4]) for i in range(5)]
            for m in range(4):
                kzj[xm, m] = sum(scaled[i] * float(DN[i, m]) for i in range(5))
        send_z(0, j)

    def advance(j, t, first):
        z_copy(t - 1, j).wait_recv()
        uj, gxj, gyj, gzj, uyj = u.at[j], gx.at[j], gy.at[j], gz.at[j], uy.at[j]
        gy4j, gz4j, kdzj, zhj = gy4.at[j], gz4.at[j], kdz.at[j], zh.at[t - 1, j]
        imj, sfj, wj, hsj = im.at[j], sf.at[j], w.at[j], hs.at[j]
        if first:
            wait_load(nat_m, j, 2)
            wait_load(nat_s, j, 3)
            wait_load(nat_v, j, 4)

        for xm in range(4):
            x = 4 * j + xm
            if first:
                for zm in range(4):
                    if xm % 2 == 0:
                        masses = apart(strided(rows_m, 16 * x + zm, 512))
                        for ym in range(4):
                            mass = masses[ym] * (TIME_STEP * TIME_STEP)
                            one, two = twice_events(mass)
                            imj[xm, 4 * zm + ym], imj[xm + 1, 4 * zm + ym] = one, two
                    values = apart(strided(rows_v, 32 * x + zm, 1024))
                    for ym in range(4):
                        wj[xm, 4 * zm + ym] = values[ym] * TIME_STEP
                    values = apart(strided(rows_s, 32 * x + zm, 1024))
                    for ym in range(4):
                        sfj[xm, 4 * zm + ym] = values[ym] * imj[xm, 4 * zm + ym]
            v = [[uj[xm, 4 * zm + ym] for ym in range(4)] for zm in range(4)]
            f = [[None] * 4 for _ in range(4)]
            arrived = zhj[xm]
            above, below = arrived * is0, arrived * is1
            for ym in range(4):
                u4 = jnp.where(radial == 3, turn(above, 3 - ym), turn(v[0][ym], 7))
                parts = line(
                    *[v[zm][ym] for zm in range(4)], u4,
                    *[gzj[xm, 4 * zm + ym] for zm in range(4)], gz4j[xm, ym],
                )
                carried = jnp.where(radial == 0, turn(below, -ym), turn(parts[4], 1))
                f[0][ym] = (parts[0] + carried) + kdzj[xm, ym] * v[0][ym]
                f[1][ym], f[3][ym] = parts[1], parts[3]
                f[2][ym] = -parts[2]
            for zm in range(4):
                parts = line(
                    *v[zm], uyj[xm, zm], *[gyj[xm, 4 * zm + ym] for ym in range(4)], gy4j[xm, zm]
                )
                fy[xm, zm] = lane_before(parts[4])
                fs[xm, 4 * zm] = f[zm][0] + parts[0]
                fs[xm, 4 * zm + 1] = f[zm][1] + parts[1]
                fs[xm, 4 * zm + 2] = f[zm][2] - parts[2]
                fs[xm, 4 * zm + 3] = f[zm][3] + parts[3]

        strength = jnp.where(upper, time_ref[0, t - 1], time_ref[1, t - 1])
        ubn, pbj, kdxj, gxn = ub.at[t - 1, j + 1], pb.at[t - 1, j], kdx.at[j], gx.at[j + 1, 0]
        for k in range(16):
            v = [uj[i, k] for i in range(4)]
            parts = line(*v, ubn[k], *[gxj[i, k] for i in range(4)], gxn[k], last=False)
            f = [
                fs[0, k] + (parts[0] + (pbj[k] + kdxj[k] * v[0])),
                fs[1, k] + parts[1],
                fs[2, k] - parts[2],
                fs[3, k] + parts[3],
            ]
            for i in range(4):
                if k % 4 == 0:
                    f[i] = f[i] + fy[i, k // 4]
                kick = strength * sfj[i, k] - imj[i, k] * f[i]
                speed = wj[i, k] + kick
                wj[i, k] = speed
                moved = v[i] + speed
                uj[i, k] = moved
                hsj[i, k] = kick * kick if first else hsj[i, k] + kick * kick
                if k % 4 == 0:
                    uyj[i, k // 4] = next_lane(moved)

    def hand_on(j, t):
        send_z(t, j)
        uj, ubj = u.at[j], ub.at[t, j]
        for k in range(16):
            ubj[k] = uj[0, k]
        partial_x(t, j)

        @pl.when(j == 0)
        def _():
            u_copy(t).start()

        @pl.when(j == 7)
        def _():
            p_copy(t).start()

    def end_copy(j, k, e):
        at = pl.ds(4 * j, 4)
        return pltpu.make_async_copy(
            nat_u.at[k, at, e], end_ref.at[e, at, :, pl.ds(128 * k, 128)], end_sem
        )

    def finish(j):
        uj, hsj = u.at[j], hs.at[j]
        for half in range(2):
            for zm in range(4):
                both = []
                for ym in range(4):
                    one, two = hsj[2 * half, 4 * zm + ym], hsj[2 * half + 1, 4 * zm + ym]
                    one = one + pltpu.roll(one, 4, 0)
                    two = two + pltpu.roll(two, 4, 0)
                    both.append(jnp.where(upper, one, two) * (100.0 / (4 * STEPS)))
                for k, value in enumerate(together(both)):
                    first = 512 * k + 16 * (4 * j + 2 * half) + zm
                    rows_sent[pl.ds(first, 8, stride=4), :] = value
        h_copy(j).start()
        for xm in range(4):
            for zm in range(4):
                whole = together([uj[xm, 4 * zm + ym] for ym in range(4)])
                for k, value in enumerate(whole):
                    rows_u[pl.ds(1024 * k + 32 * (4 * j + xm) + zm, 8, stride=4), :] = value
        for k in range(4):
            for e in range(2):
                end_copy(j, k, e).start()

    @pl.loop(0, len(ORDER))
    def _(n):
        j = digit(n, [j for j, _ in ORDER], 4)
        t = digit(n, [t for _, t in ORDER], 4)

        @pl.when(t == 1)
        def _():
            @pl.when(j == 0)
            def _():
                layer_copy().wait_recv()
                for k in range(16):
                    own = gx[0, 0, k] * float(DN[4, 4])
                    pb[0, 0, k] = layer[3, k] + own * layer[4, k]
                    kdx[0, k] = layer[5, k] + own * float(DN[4, 4])

            @pl.when(j == 7)
            def _():
                u_copy(0).wait_recv()
                g_copy().wait_recv()
                next_coefs(7)

            advance(j, t, True)
            hand_on(j, t)

        @pl.when(t > 1)
        def _():
            @pl.when(j == 0)
            def _():
                p_copy(t - 1).wait_recv()

            @pl.when(j == 7)
            def _():
                u_copy(t - 1).wait_recv()

            advance(j, t, False)

            @pl.when(t < STEPS)
            def _():
                hand_on(j, t)

            @pl.when(t == STEPS)
            def _():
                finish(j)

    @pl.loop(0, 8)
    def _(n):
        j = digit(n, LAST_ORDER, 4)
        h_copy(j).wait_recv()
        for xm in range(4):
            x = 4 * j + xm
            for k in range(4):
                hessian_ref[x, :, pl.ds(128 * k, 128)] = sent[k, x] + got[k, x]

    u_copy(0).wait_send()
    g_copy().wait_send()
    layer_copy().wait_send()
    gz_copy(0, 8).wait_send()
    for t in range(1, 4):
        u_copy(t).wait_send()
        p_copy(t).wait_send()

    @pl.loop(0, 8)
    def _(j):
        h_copy(j).wait_send()

    pltpu.make_async_copy(zs, zs, zsend).wait()
    pltpu.make_async_copy(nat_u, nat_u, end_sem).wait()


def per_device(slabs, blocks, *arrays):
    anywhere = pl.BlockSpec(memory_space=pl.ANY)
    inside = pl.BlockSpec(memory_space=pltpu.VMEM)

    def tiles(*shape):
        return pltpu.VMEM((*shape, 8, 128), jnp.float32)

    field, natural = tiles(8, 4, 16), pltpu.VMEM((4, 32, 16, 128), jnp.float32)
    natural_events = pltpu.VMEM((4, 32, 2, 16, 128), jnp.float32)
    several = pltpu.SemaphoreType.DMA
    scratch = [
        natural_events, natural_events, natural_events,
        natural, natural, pltpu.VMEM((32, 512), jnp.int32),
        field, field, field, field, field,
        tiles(9, 4, 16), field, field,
        tiles(8, 4, 4), tiles(8, 4, 4), tiles(8, 4, 4),
        tiles(8, 4, 16), tiles(9, 16), tiles(8, 4, 4), tiles(8, 4, 4),
        tiles(4, 9, 16), tiles(4, 9, 16), tiles(4, 16), tiles(4, 4),
        tiles(4, 8, 4), tiles(4, 8, 4), tiles(8, 4), tiles(8, 4),
        tiles(6, 16), pltpu.VMEM((4, 32, 128), jnp.int32),
        natural, natural, pltpu.VMEM((8, 8, 128), jnp.int32),
        several((8, 5)), several, several, several((4, 8)),
        several, several, several, several,
        several((4,)), several((4,)), several((4,)), several((4,)),
        several, several, several((8,)), several((8,)),
    ]
    results = pl.pallas_call(
        functools.partial(body, slabs, blocks),
        out_shape=(
            pltpu.VMEM((2, 32, 16, 512), jnp.float32),
            pltpu.VMEM((32, 16, 512), jnp.float32),
        ),
        in_specs=[anywhere] * 3 + [pl.BlockSpec(memory_space=pltpu.SMEM)] + [anywhere] * 3,
        out_specs=(inside, inside),
        scratch_shapes=scratch,
        compiler_params=pltpu.CompilerParams(
            collective_id=0, has_side_effects=True, vmem_limit_bytes=56 << 20
        ),
        name="adjoint_steps",
    )(*arrays)
    return pl.pallas_call(
        place_out,
        out_shape=(
            jax.ShapeDtypeStruct((2, 32, 16, 512), jnp.float32),
            jax.ShapeDtypeStruct((32, 16, 512), jnp.float32),
        ),
        in_specs=[anywhere] * 2,
        out_specs=(anywhere, anywhere),
        scratch_shapes=[several((6,))],
        name="place_out",
    )(*results)


def solution(mesh):
    in_specs = (
        P("event", "block", "slab", None),
        P("event", "block", "slab", None),
        P("event", "block", "slab", None),
        P("event", None),
        P("block", "slab", None),
        P("block", "slab", None),
        P("block", None),
    )
    out_specs = (P("event", "block", "slab", None), P("block", "slab", None))
    return jax.shard_map(
        functools.partial(per_device, mesh.shape["slab"], mesh.shape["block"]),
        mesh=mesh, in_specs=in_specs, out_specs=out_specs, check_vma=False,
    )
```

```python
import functools

import jax
import jax.numpy as jnp
import numpy as np
from jax import lax
from jax.experimental import pallas as pl
from jax.experimental.pallas import tpu as pltpu
from jax.sharding import PartitionSpec as P

STEPS = 4
TIME_STEP = 0.1
CRUST_FACTOR = 0.35
WEIGHTS = (0.1, 49.0 / 90.0, 32.0 / 45.0, 49.0 / 90.0, 0.1)
ASSEMBLED = (0.2, 49.0 / 90.0, 32.0 / 45.0, 49.0 / 90.0)
MESH = pl.DeviceIdType.MESH
TILE = (8, 128)


def derivative_table():
    points = np.array([-1.0, -np.sqrt(3.0 / 7.0), 0.0, np.sqrt(3.0 / 7.0), 1.0])
    scales = np.array(
        [
            np.prod([points[one] - points[other] for other in range(5) if other != one])
            for one in range(5)
        ]
    )
    table = np.zeros((5, 5))
    for target in range(5):
        for anchor in range(5):
            if target != anchor:
                table[target, anchor] = scales[target] / (
                    scales[anchor] * (points[target] - points[anchor])
                )
        table[target, target] = -np.sum(table[target])
    return table


D = derivative_table()
A4, B4 = (D[4, 4] - D[4, 0]) / 2, (D[4, 3] - D[4, 1]) / 2
E4, T4 = (D[4, 4] + D[4, 0]) / 2, (D[4, 3] + D[4, 1]) / 2
A3, B3 = (D[3, 4] - D[3, 0]) / 2, (D[3, 3] - D[3, 1]) / 2
E3, T3 = (D[3, 4] + D[3, 0]) / 2, (D[3, 3] + D[3, 1]) / 2
SCALE = (A4, A3, D[2, 3], A3, A4)
DN = D / np.array(SCALE)[:, None]
KAPPA0, GAMMA, DELTA = B4 / A4, E4 / A4, T4 / A4
KAPPA1, EPSILON, ZETA = B3 / A3, E3 / A3, T3 / A3
KAPPA2 = D[2, 4] / D[2, 3]
RHO = [WEIGHTS[i] * SCALE[i] ** 2 for i in range(5)]


def line(u0, u1, u2, u3, u4, c0, c1, c2, c3, c4, last=True):
    a, b = u4 - u0, u3 - u1
    twice = u2 + u2
    e, f = (u4 + u0) - twice, (u3 + u1) - twice
    p, q = a + KAPPA0 * b, GAMMA * e + DELTA * f
    r, s = a + KAPPA1 * b, EPSILON * e + ZETA * f
    h4, h0 = (p + q) * c4, (p - q) * c0
    h3, h1 = (r + s) * c3, (r - s) * c1
    h2 = (b + KAPPA2 * a) * c2
    hp, hm = h4 + h0, h4 - h0
    ep, em = h3 + h1, h3 - h1
    fa = (hp + ep) + KAPPA2 * h2
    fb = (KAPPA0 * hp + KAPPA1 * ep) + h2
    fe = GAMMA * hm + EPSILON * em
    ff = DELTA * hm + ZETA * em
    total = fe + ff
    return fe - fa, ff - fb, total + total, ff + fb, (fe + fa if last else None)


ORDER = (
    (4, 1), (3, 1), (2, 1), (1, 1), (7, 1), (2, 2), (0, 1), (6, 1), (5, 1), (3, 2), (4, 2), (1, 2),
    (2, 3), (0, 2), (1, 3), (7, 2), (3, 3), (2, 4), (5, 2), (6, 2), (4, 3), (3, 4), (6, 3), (0, 3),
    (5, 3), (1, 4), (7, 3), (5, 4), (4, 4), (6, 4), (0, 4), (7, 4),
)
ORDER_OF_FIRST = (
    (4, 1), (3, 1), (5, 1), (2, 1), (6, 1), (1, 1), (3, 2), (4, 2), (5, 2), (2, 2), (4, 3), (3, 3),
    (7, 1), (6, 2), (5, 3), (4, 4), (0, 1), (1, 2), (2, 3), (3, 4), (7, 2), (6, 3), (5, 4), (0, 2),
    (1, 3), (2, 4), (7, 3), (6, 4), (0, 3), (1, 4), (7, 4), (0, 4),
)


def digit(n, digits, bits):
    words = [
        sum(d << (bits * i) for i, d in enumerate(digits[s : s + 7])) for s in range(0, len(digits), 7)
    ]
    word, place = words[0], n
    for i in range(1, len(words)):
        word = jnp.where(n < 7 * i, word, words[i])
        place = jnp.where(n < 7 * i, place, n - 7 * i)
    return (word >> (bits * place)) & ((1 << bits) - 1)


def body(slabs, blocks, *refs):
    (
        start_hbm, velocity_hbm, source_hbm, time_ref, modulus_hbm, mass_hbm, crust_hbm,
        end_ref, hessian_ref,
        nat_u, nat_v, nat_s, nat_g, nat_m, nat_c,
        u, w, sf, im, hs, gx, gy, gz, uy, gy4, gz4, kx, kdx, kz, kdz, ub, pb, fs, fy,
        zs, zh, gzs, gzh, layer, crust, sent, got, index,
        in_sem, end_sem, zsend, zrecv, gzsend, gzrecv, gsend, grecv,
        usend, urecv, psend, precv, qsend, qrecv, hsend, hrecv, ready,
    ) = refs
    block = lax.axis_index("block")
    slab = lax.axis_index("slab")
    event = lax.axis_index("event")
    before = (lax.rem(block + blocks - 1, blocks), slab, event)
    after = (lax.rem(block + 1, blocks), slab, event)
    other_slab = (block, 1 - slab, event)
    other_event = (block, slab, 1 - event)

    plane = 8
    late = lax.rem(block, plane) == 0
    last = lax.rem(block, plane) == plane - 1
    barrier = pltpu.get_barrier_semaphore()
    for device in (before, other_slab, other_event):
        pl.semaphore_signal(barrier, inc=1, device_id=device, device_id_type=MESH)

    @pl.when(jnp.logical_not(last))
    def _():
        pl.semaphore_signal(barrier, inc=1, device_id=after, device_id_type=MESH)

    groups = ((0, 1), (7, 1), (1, 6))

    def start_early(group):
        first, count = groups[group]
        at = pl.ds(4 * first, 4 * count)
        for k in range(4):
            lanes = (slice(None), pl.ds(128 * k, 128))
            pairs = [(modulus_hbm.at[at, *lanes], nat_g.at[k, at], 0)]
            for e in range(2):
                pairs.append((start_hbm.at[e, at, *lanes], nat_u.at[k, at, e], 1))
            for source, target, kind in pairs:
                pltpu.make_async_copy(source, target, in_sem.at[kind, group]).start()

    def wait_early(group):
        first, count = groups[group]
        for kind, ref in enumerate((nat_g, nat_u)):
            part = ref.at[:, pl.ds(4 * first, 4 * count)]
            pltpu.make_async_copy(part, part, in_sem.at[kind, group]).wait()

    def start_late():
        for k in range(4):
            lanes = (slice(None), slice(None), pl.ds(128 * k, 128))
            pairs = [(mass_hbm.at[*lanes], nat_m.at[k], 0)]
            for e in range(2):
                pairs.append((source_hbm.at[e, *lanes], nat_s.at[k, :, e], 1))
                pairs.append((velocity_hbm.at[e, *lanes], nat_v.at[k, :, e], 2))
            for source, target, kind in pairs:
                pltpu.make_async_copy(source, target, in_sem.at[2, kind]).start()

    def wait_late():
        for kind, ref in enumerate((nat_m, nat_s, nat_v)):
            pltpu.make_async_copy(ref, ref, in_sem.at[2, kind]).wait()

    crust_load = pltpu.make_async_copy(crust_hbm, nat_c, gsend)
    crust_load.start()

    for group in range(3):
        start_early(group)
    start_late()

    lane = lax.broadcasted_iota(jnp.int32, TILE, 1)
    row = lax.broadcasted_iota(jnp.int32, TILE, 0)
    radial = row & 3
    for r in range(4):
        index[r] = 4 * (lane & 31) + ((r - (lane >> 5)) & 3)
        index[4 + r] = 32 * ((r - (lane & 3)) & 3) + (lane >> 2)
    bit0, bit1 = (lane & 1) == 1, (lane & 2) == 2
    block0, block1 = (lane & 32) == 32, (lane & 64) == 64
    upper = row < 4
    is0 = jnp.where(slab == 0, 1.0, 0.0).astype(jnp.float32)
    is1 = 1.0 - is0

    def gather(value, k):
        return jnp.take_along_axis(value, index[k], axis=1)

    def apart(t):
        x = [jnp.where(bit0, t[(r + 3) % 4], t[r]) for r in range(4)]
        m = [jnp.where(bit1, x[(r + 2) % 4], x[r]) for r in range(4)]
        n = [gather(m[r], r) for r in range(4)]
        y = [jnp.where(block0, n[(k + 1) % 4], n[k]) for k in range(4)]
        return [jnp.where(block1, y[(k + 2) % 4], y[k]) for k in range(4)]

    def together(o):
        y = [jnp.where(block0, o[(r + 3) % 4], o[r]) for r in range(4)]
        n = [jnp.where(block1, y[(r + 2) % 4], y[r]) for r in range(4)]
        m = [gather(n[r], 4 + r) for r in range(4)]
        z = [jnp.where(bit0, m[(k + 1) % 4], m[k]) for k in range(4)]
        return [jnp.where(bit1, z[(k + 2) % 4], z[k]) for k in range(4)]

    def turn(value, shift):
        return value if shift % 8 == 0 else pltpu.roll(value, shift % 8, 0)

    def pack(values, at):
        result = turn(values[0], -at)
        for k in range(1, 4):
            result = jnp.where(radial == k, turn(values[k], k - at), result)
        return result

    def next_lane(value):
        return jnp.where(lane == 127, 0.0, pltpu.roll(value, 127, 1))

    def lane_before(value):
        return jnp.where(lane == 0, 0.0, pltpu.roll(value, 1, 1))

    def twice_events(value):
        other = pltpu.roll(value, 4, 0)
        return jnp.where(upper, value, other), jnp.where(upper, other, value)

    def rows_of(ref, per):
        return ref.reshape(4 * 32 * per, 128)

    rows_u, rows_v, rows_s = rows_of(nat_u, 32), rows_of(nat_v, 32), rows_of(nat_s, 32)
    rows_g, rows_m, rows_sent = rows_of(nat_g, 16), rows_of(nat_m, 16), rows_of(sent, 16)

    def strided(ref, first, count):
        return [ref[pl.ds(first + count * k, 8, stride=4), :] for k in range(4)]

    edge_z = jnp.where(slab == 0, jnp.where(radial == 0, 0.1, 0.2), 0.2).astype(jnp.float32)
    edge_y = jnp.where(lane == 0, 0.1, 0.2).astype(jnp.float32)

    def over_z(value, zm):
        return value * (edge_z if zm == 0 else ASSEMBLED[zm])

    def over_y(value, ym):
        return value * (edge_y if ym == 0 else ASSEMBLED[ym])

    crust_load.wait()

    @pl.loop(0, 4)
    def _(part):
        at = pl.ds(pl.multiple_of(8 * part, 8), 8)
        found = apart([nat_c[at, pl.ds(128 * k, 128)] for k in range(4)])
        for k in range(4):
            crust[k, at, :] = found[k]

    def set_up(j):
        gxj, gyj, gzj = gx.at[j], gy.at[j], gz.at[j]
        for half in range(2):
            x = 4 * j + 2 * half
            depth = [
                jnp.where(
                    upper,
                    jnp.broadcast_to(crust[ym, pl.ds(x, 1), :], TILE),
                    jnp.broadcast_to(crust[ym, pl.ds(x + 1, 1), :], TILE),
                )
                for ym in range(4)
            ]
            for zm in range(4):
                moduli = apart(strided(rows_g, 16 * x + zm, 512))
                place = slab * 16 + 4 * radial + zm
                for ym in range(4):
                    stiff = jnp.where(
                        place >= 16 * slabs - depth[ym], CRUST_FACTOR * moduli[ym], moduli[ym]
                    )
                    at = 4 * zm + ym
                    for side, value in enumerate(twice_events(stiff)):
                        xm = 2 * half + side
                        in_y, in_z = over_y(value, ym), over_z(value, zm)
                        gxj[xm, at] = over_z(in_y, zm) * RHO[xm]
                        gyj[xm, at] = in_z * (RHO[ym] * ASSEMBLED[xm])
                        gzj[xm, at] = in_y * (RHO[zm] * ASSEMBLED[xm])
        for xm in range(4):
            for zm in range(4):
                gy4[j, xm, zm] = next_lane(gyj[xm, 4 * zm])
        uj, ubj, uyj = u.at[j], ub.at[0, j], uy.at[j]
        for xm in range(4):
            x = 4 * j + xm
            for zm in range(4):
                values = apart(strided(rows_u, 32 * x + zm, 1024))
                for ym in range(4):
                    uj[xm, 4 * zm + ym] = values[ym]
                    if xm == 0:
                        ubj[4 * zm + ym] = values[ym]
                uyj[xm, zm] = next_lane(values[0])
        for xm in range(4):
            first = pack([gzj[xm, ym] for ym in range(4)], 0)
            ends = [pack([gzj[xm, 4 * zm + ym] for ym in range(4)], 3) for zm in range(4)]
            for zm in range(4):
                kz[j, xm, zm] = ends[zm]
            total = sum(ends[zm] * float(DN[zm, 4] ** 2) for zm in range(4))
            gzs[j, xm] = is0 * total + is1 * first

    def gz_copy(j, count=1):
        at = pl.ds(j, count)
        return pltpu.make_async_remote_copy(
            src_ref=gzs.at[at], dst_ref=gzh.at[at], send_sem=gzsend, recv_sem=gzrecv,
            device_id=other_slab, device_id_type=MESH,
        )

    def z_copy(t, j):
        return pltpu.make_async_remote_copy(
            src_ref=zs.at[t, j], dst_ref=zh.at[t, j], send_sem=zsend, recv_sem=zrecv.at[t, j],
            device_id=other_slab, device_id_type=MESH,
        )

    def u_copy(t):
        return pltpu.make_async_remote_copy(
            src_ref=ub.at[t, 0], dst_ref=ub.at[t, 8], send_sem=usend.at[t], recv_sem=urecv.at[t],
            device_id=before, device_id_type=MESH,
        )

    def g_copy():
        return pltpu.make_async_remote_copy(
            src_ref=gx.at[0, 0], dst_ref=gx.at[8, 0], send_sem=gsend, recv_sem=grecv,
            device_id=before, device_id_type=MESH,
        )

    def p_copy(t):
        return pltpu.make_async_remote_copy(
            src_ref=pb.at[t, 8], dst_ref=pb.at[t, 0], send_sem=psend.at[t], recv_sem=precv.at[t],
            device_id=after, device_id_type=MESH,
        )

    def layer_copy():
        return pltpu.make_async_remote_copy(
            src_ref=layer.at[pl.ds(0, 3)], dst_ref=layer.at[pl.ds(3, 3)], send_sem=qsend, recv_sem=qrecv,
            device_id=after, device_id_type=MESH,
        )

    def h_copy(j):
        at = pl.ds(4 * j, 4)
        return pltpu.make_async_remote_copy(
            src_ref=sent.at[:, at], dst_ref=got.at[:, at], send_sem=hsend.at[j], recv_sem=hrecv.at[j],
            device_id=other_event, device_id_type=MESH,
        )

    @pl.loop(0, 8)
    def _(n):
        j = lax.rem(7 * n, 8)
        for group in range(3):

            @pl.when(n == group)
            def _():
                wait_early(group)

        set_up(j)

        @pl.when(n == 0)
        def _():
            @pl.when(late)
            def _():
                pl.semaphore_wait(barrier, 3)

            @pl.when(jnp.logical_not(late))
            def _():
                pl.semaphore_wait(barrier, 4)
                u_copy(0).start()
                g_copy().start()

            @pl.when(last)
            def _():
                pl.semaphore_signal(ready, inc=1, device_id=after, device_id_type=MESH)

        gz_copy(j).start()

        @pl.when(n == 1)
        def _():
            for k in range(16):
                g = [gx[7, i, k] for i in range(4)]
                v = [u[7, i, k] for i in range(4)]
                scaled = [g[i] * float(DN[i, 4]) for i in range(4)]
                layer[2, k] = sum(scaled[i] * float(DN[i, 4]) for i in range(4))
                layer[0, k] = sum(
                    scaled[i] * sum(float(DN[i, m]) * v[m] for m in range(4)) for i in range(4)
                )
                layer[1, k] = sum(float(DN[4, m]) * v[m] for m in range(4))
            layer_copy().start()

    def next_coefs(j):
        gj, gn, kj, kn = gx.at[j], gx.at[j + 1, 0], kx.at[j], kdx.at[j + 1]
        for k in range(16):
            scaled = [gj[i, k] * float(DN[i, 4]) for i in range(4)] + [gn[k] * float(DN[4, 4])]
            for m in range(4):
                kj[m, k] = sum(scaled[i] * float(DN[i, m]) for i in range(5))
            kn[k] = sum(scaled[i] * float(DN[i, 4]) for i in range(5))

    def partial_x(t, j):
        uj, kj, pj = u.at[j], kx.at[j], pb.at[t, j + 1]
        for k in range(16):
            pj[k] = (kj[0, k] * uj[0, k] + kj[1, k] * uj[1, k]) + (
                kj[2, k] * uj[2, k] + kj[3, k] * uj[3, k]
            )

    @pl.loop(0, 7)
    def _(j):
        next_coefs(j)
        partial_x(0, j)

    def send_z(t, j):
        uj, zj = u.at[j], zs.at[t, j]

        @pl.when(slab == 0)
        def _():
            kj = kz.at[j]
            for xm in range(4):
                packed = [pack([uj[xm, 4 * zm + ym] for ym in range(4)], 3) for zm in range(4)]
                zj[xm] = (kj[xm, 0] * packed[0] + kj[xm, 1] * packed[1]) + (
                    kj[xm, 2] * packed[2] + kj[xm, 3] * packed[3]
                )

        @pl.when(slab != 0)
        def _():
            for xm in range(4):
                zj[xm] = pack([uj[xm, ym] for ym in range(4)], 0)

        z_copy(t, j).start()

    gz_copy(0, 8).wait_recv()

    @pl.loop(0, 8)
    def _(n):
        j = lax.rem(n + 1, 8)
        gzj, gz4j, kzj, kdzj, gzhj = gz.at[j], gz4.at[j], kz.at[j], kdz.at[j], gzh.at[j]
        for xm in range(4):
            arrived = gzhj[xm]
            above, below = arrived * is0, arrived * is1
            for ym in range(4):
                own = gzj[xm, ym]
                gz4j[xm, ym] = jnp.where(radial == 3, turn(above, 3 - ym), turn(own, 7))
                diagonal = turn(below, -ym) + is1 * float(DN[4, 4] ** 2) * own
                kdzj[xm, ym] = jnp.where(radial == 0, diagonal, 0.0)
            ends = [kzj[xm, zm] for zm in range(4)] + [arrived]
            scaled = [ends[i] * float(DN[i, 4]) for i in range(5)]
            for m in range(4):
                kzj[xm, m] = sum(scaled[i] * float(DN[i, m]) for i in range(5))
        send_z(0, j)

    def advance(j, t, first):
        z_copy(t - 1, j).wait_recv()
        uj, gxj, gyj, gzj, uyj = u.at[j], gx.at[j], gy.at[j], gz.at[j], uy.at[j]
        gy4j, gz4j, kdzj, zhj = gy4.at[j], gz4.at[j], kdz.at[j], zh.at[t - 1, j]
        imj, sfj, wj, hsj = im.at[j], sf.at[j], w.at[j], hs.at[j]

        for xm in range(4):
            x = 4 * j + xm
            if first:
                for zm in range(4):
                    if xm % 2 == 0:
                        masses = apart(strided(rows_m, 16 * x + zm, 512))
                        for ym in range(4):
                            mass = masses[ym] * (TIME_STEP * TIME_STEP)
                            one, two = twice_events(mass)
                            imj[xm, 4 * zm + ym], imj[xm + 1, 4 * zm + ym] = one, two
                    values = apart(strided(rows_v, 32 * x + zm, 1024))
                    for ym in range(4):
                        wj[xm, 4 * zm + ym] = values[ym] * TIME_STEP
                    values = apart(strided(rows_s, 32 * x + zm, 1024))
                    for ym in range(4):
                        sfj[xm, 4 * zm + ym] = values[ym] * imj[xm, 4 * zm + ym]
            v = [[uj[xm, 4 * zm + ym] for ym in range(4)] for zm in range(4)]
            f = [[None] * 4 for _ in range(4)]
            arrived = zhj[xm]
            above, below = arrived * is0, arrived * is1
            for ym in range(4):
                u4 = jnp.where(radial == 3, turn(above, 3 - ym), turn(v[0][ym], 7))
                parts = line(
                    *[v[zm][ym] for zm in range(4)], u4,
                    *[gzj[xm, 4 * zm + ym] for zm in range(4)], gz4j[xm, ym],
                )
                carried = jnp.where(radial == 0, turn(below, -ym), turn(parts[4], 1))
                f[0][ym] = (parts[0] + carried) + kdzj[xm, ym] * v[0][ym]
                f[1][ym], f[3][ym] = parts[1], parts[3]
                f[2][ym] = -parts[2]
            for zm in range(4):
                parts = line(
                    *v[zm], uyj[xm, zm], *[gyj[xm, 4 * zm + ym] for ym in range(4)], gy4j[xm, zm]
                )
                fy[xm, zm] = lane_before(parts[4])
                fs[xm, 4 * zm] = f[zm][0] + parts[0]
                fs[xm, 4 * zm + 1] = f[zm][1] + parts[1]
                fs[xm, 4 * zm + 2] = f[zm][2] - parts[2]
                fs[xm, 4 * zm + 3] = f[zm][3] + parts[3]

        strength = jnp.where(upper, time_ref[0, t - 1], time_ref[1, t - 1])
        ubn, pbj, kdxj, gxn = ub.at[t - 1, j + 1], pb.at[t - 1, j], kdx.at[j], gx.at[j + 1, 0]
        for k in range(16):
            v = [uj[i, k] for i in range(4)]
            parts = line(*v, ubn[k], *[gxj[i, k] for i in range(4)], gxn[k], last=False)
            f = [
                fs[0, k] + (parts[0] + (pbj[k] + kdxj[k] * v[0])),
                fs[1, k] + parts[1],
                fs[2, k] - parts[2],
                fs[3, k] + parts[3],
            ]
            for i in range(4):
                if k % 4 == 0:
                    f[i] = f[i] + fy[i, k // 4]
                kick = strength * sfj[i, k] - imj[i, k] * f[i]
                speed = wj[i, k] + kick
                wj[i, k] = speed
                moved = v[i] + speed
                uj[i, k] = moved
                hsj[i, k] = kick * kick if first else hsj[i, k] + kick * kick
                if k % 4 == 0:
                    uyj[i, k // 4] = next_lane(moved)

    def hand_on(j, t):
        send_z(t, j)
        uj, ubj = u.at[j], ub.at[t, j]
        for k in range(16):
            ubj[k] = uj[0, k]
        partial_x(t, j)

        @pl.when(j == 0)
        def _():
            u_copy(t).start()

        @pl.when(j == 7)
        def _():
            p_copy(t).start()

    def end_copy(j, k, e):
        at = pl.ds(4 * j, 4)
        return pltpu.make_async_copy(
            nat_u.at[k, at, e], end_ref.at[e, at, :, pl.ds(128 * k, 128)], end_sem
        )

    def finish(j):
        uj, hsj = u.at[j], hs.at[j]
        for half in range(2):
            for zm in range(4):
                both = []
                for ym in range(4):
                    one, two = hsj[2 * half, 4 * zm + ym], hsj[2 * half + 1, 4 * zm + ym]
                    one = one + pltpu.roll(one, 4, 0)
                    two = two + pltpu.roll(two, 4, 0)
                    both.append(jnp.where(upper, one, two) * (100.0 / (4 * STEPS)))
                for k, value in enumerate(together(both)):
                    first = 512 * k + 16 * (4 * j + 2 * half) + zm
                    rows_sent[pl.ds(first, 8, stride=4), :] = value
        h_copy(j).start()
        for xm in range(4):
            for zm in range(4):
                whole = together([uj[xm, 4 * zm + ym] for ym in range(4)])
                for k, value in enumerate(whole):
                    rows_u[pl.ds(1024 * k + 32 * (4 * j + xm) + zm, 8, stride=4), :] = value
        for k in range(4):
            for e in range(2):
                end_copy(j, k, e).start()

    wait_late()

    @pl.loop(0, len(ORDER))
    def _(n):
        j, t = [
            jnp.where(block == 0, digit(n, [task[i] for task in ORDER_OF_FIRST], 4), digit(n, [task[i] for task in ORDER], 4))
            for i in range(2)
        ]

        @pl.when(jnp.logical_and(late, n == jnp.where(block == 0, 4, 0)))
        def _():
            pl.semaphore_wait(ready, 1)
            u_copy(0).start()
            g_copy().start()

        @pl.when(t == 1)
        def _():
            @pl.when(j == 0)
            def _():
                layer_copy().wait_recv()
                for k in range(16):
                    own = gx[0, 0, k] * float(DN[4, 4])
                    pb[0, 0, k] = layer[3, k] + own * layer[4, k]
                    kdx[0, k] = layer[5, k] + own * float(DN[4, 4])

            @pl.when(j == 7)
            def _():
                u_copy(0).wait_recv()
                g_copy().wait_recv()
                next_coefs(7)

            advance(j, t, True)
            hand_on(j, t)

        @pl.when(t > 1)
        def _():
            @pl.when(j == 0)
            def _():
                p_copy(t - 1).wait_recv()

            @pl.when(j == 7)
            def _():
                u_copy(t - 1).wait_recv()

            advance(j, t, False)

            @pl.when(t < STEPS)
            def _():
                hand_on(j, t)

            @pl.when(t == STEPS)
            def _():
                finish(j)

    @pl.loop(0, 8)
    def _(n):
        j = jnp.where(
            block == 0, *[digit(n, [j for j, t in order if t == STEPS], 4) for order in (ORDER_OF_FIRST, ORDER)]
        )
        h_copy(j).wait_recv()
        for xm in range(4):
            x = 4 * j + xm
            for k in range(4):
                hessian_ref[x, :, pl.ds(128 * k, 128)] = sent[k, x] + got[k, x]

    u_copy(0).wait_send()
    g_copy().wait_send()
    layer_copy().wait_send()
    gz_copy(0, 8).wait_send()
    for t in range(1, 4):
        u_copy(t).wait_send()
        p_copy(t).wait_send()

    @pl.loop(0, 8)
    def _(j):
        h_copy(j).wait_send()

    pltpu.make_async_copy(zs, zs, zsend).wait()
    pltpu.make_async_copy(nat_u, nat_u, end_sem).wait()


def per_device(slabs, blocks, *arrays):
    anywhere = pl.BlockSpec(memory_space=pl.ANY)
    inside = pl.BlockSpec(memory_space=pltpu.VMEM)

    def tiles(*shape):
        return pltpu.VMEM((*shape, 8, 128), jnp.float32)

    field, natural = tiles(8, 4, 16), pltpu.VMEM((4, 32, 16, 128), jnp.float32)
    natural_events = pltpu.VMEM((4, 32, 2, 16, 128), jnp.float32)
    several = pltpu.SemaphoreType.DMA
    scratch = [
        natural_events, natural_events, natural_events,
        natural, natural, pltpu.VMEM((32, 512), jnp.int32),
        field, field, field, field, field,
        tiles(9, 4, 16), field, field,
        tiles(8, 4, 4), tiles(8, 4, 4), tiles(8, 4, 4),
        tiles(8, 4, 16), tiles(9, 16), tiles(8, 4, 4), tiles(8, 4, 4),
        tiles(4, 9, 16), tiles(4, 9, 16), tiles(4, 16), tiles(4, 4),
        tiles(4, 8, 4), tiles(4, 8, 4), tiles(8, 4), tiles(8, 4),
        tiles(6, 16), pltpu.VMEM((4, 32, 128), jnp.int32),
        natural, natural, pltpu.VMEM((8, 8, 128), jnp.int32),
        several((3, 3)), several, several, several((4, 8)),
        several, several, several, several,
        several((4,)), several((4,)), several((4,)), several((4,)),
        several, several, several((8,)), several((8,)),
        pltpu.SemaphoreType.REGULAR,
    ]
    return pl.pallas_call(
        functools.partial(body, slabs, blocks),
        out_shape=(
            pltpu.VMEM((2, 32, 16, 512), jnp.float32),
            pltpu.VMEM((32, 16, 512), jnp.float32),
        ),
        in_specs=[anywhere] * 3 + [pl.BlockSpec(memory_space=pltpu.SMEM)] + [anywhere] * 3,
        out_specs=(inside, inside),
        scratch_shapes=scratch,
        compiler_params=pltpu.CompilerParams(
            collective_id=0, has_side_effects=True, vmem_limit_bytes=56 << 20
        ),
        name="adjoint_steps",
    )(*arrays)


def solution(mesh):
    in_specs = (
        P("event", "block", "slab", None),
        P("event", "block", "slab", None),
        P("event", "block", "slab", None),
        P("event", None),
        P("block", "slab", None),
        P("block", "slab", None),
        P("block", None),
    )
    out_specs = (P("event", "block", "slab", None), P("block", "slab", None))
    return jax.shard_map(
        functools.partial(per_device, mesh.shape["slab"], mesh.shape["block"]),
        mesh=mesh, in_specs=in_specs, out_specs=out_specs, check_vma=False,
    )
```

```python
import functools

import jax
import jax.numpy as jnp
import numpy as np
from jax import lax
from jax.experimental import pallas as pl
from jax.experimental.pallas import tpu as pltpu
from jax.sharding import PartitionSpec as P

STEPS = 4
TIME_STEP = 0.1
CRUST_FACTOR = 0.35
WEIGHTS = (0.1, 49.0 / 90.0, 32.0 / 45.0, 49.0 / 90.0, 0.1)
ASSEMBLED = (0.2, 49.0 / 90.0, 32.0 / 45.0, 49.0 / 90.0)
MESH = pl.DeviceIdType.MESH
TILE = (8, 128)


def derivative_table():
    points = np.array([-1.0, -np.sqrt(3.0 / 7.0), 0.0, np.sqrt(3.0 / 7.0), 1.0])
    scales = np.array(
        [
            np.prod([points[one] - points[other] for other in range(5) if other != one])
            for one in range(5)
        ]
    )
    table = np.zeros((5, 5))
    for target in range(5):
        for anchor in range(5):
            if target != anchor:
                table[target, anchor] = scales[target] / (
                    scales[anchor] * (points[target] - points[anchor])
                )
        table[target, target] = -np.sum(table[target])
    return table


D = derivative_table()
A4, B4 = (D[4, 4] - D[4, 0]) / 2, (D[4, 3] - D[4, 1]) / 2
E4, T4 = (D[4, 4] + D[4, 0]) / 2, (D[4, 3] + D[4, 1]) / 2
A3, B3 = (D[3, 4] - D[3, 0]) / 2, (D[3, 3] - D[3, 1]) / 2
E3, T3 = (D[3, 4] + D[3, 0]) / 2, (D[3, 3] + D[3, 1]) / 2
SCALE = (A4, A3, D[2, 3], A3, A4)
DN = D / np.array(SCALE)[:, None]
KAPPA0, GAMMA, DELTA = B4 / A4, E4 / A4, T4 / A4
KAPPA1, EPSILON, ZETA = B3 / A3, E3 / A3, T3 / A3
KAPPA2 = D[2, 4] / D[2, 3]
RHO = [WEIGHTS[i] * SCALE[i] ** 2 for i in range(5)]


def line(u0, u1, u2, u3, u4, c0, c1, c2, c3, c4, last=True):
    a, b = u4 - u0, u3 - u1
    twice = u2 + u2
    e, f = (u4 + u0) - twice, (u3 + u1) - twice
    p, q = a + KAPPA0 * b, GAMMA * e + DELTA * f
    r, s = a + KAPPA1 * b, EPSILON * e + ZETA * f
    h4, h0 = (p + q) * c4, (p - q) * c0
    h3, h1 = (r + s) * c3, (r - s) * c1
    h2 = (b + KAPPA2 * a) * c2
    hp, hm = h4 + h0, h4 - h0
    ep, em = h3 + h1, h3 - h1
    fa = (hp + ep) + KAPPA2 * h2
    fb = (KAPPA0 * hp + KAPPA1 * ep) + h2
    fe = GAMMA * hm + EPSILON * em
    ff = DELTA * hm + ZETA * em
    total = fe + ff
    return fe - fa, ff - fb, total + total, ff + fb, (fe + fa if last else None)


ORDER = (
    (4, 1), (3, 1), (2, 1), (1, 1), (7, 1), (2, 2), (0, 1), (6, 1), (5, 1), (3, 2), (4, 2), (1, 2),
    (2, 3), (0, 2), (1, 3), (7, 2), (3, 3), (2, 4), (5, 2), (6, 2), (4, 3), (3, 4), (6, 3), (0, 3),
    (5, 3), (1, 4), (7, 3), (5, 4), (4, 4), (6, 4), (0, 4), (7, 4),
)
ORDER_OF_FIRST = (
    (4, 1), (3, 1), (5, 1), (2, 1), (6, 1), (1, 1), (3, 2), (4, 2), (5, 2), (2, 2), (4, 3), (3, 3),
    (7, 1), (6, 2), (5, 3), (4, 4), (0, 1), (1, 2), (2, 3), (3, 4), (7, 2), (6, 3), (5, 4), (0, 2),
    (1, 3), (2, 4), (7, 3), (6, 4), (0, 3), (1, 4), (7, 4), (0, 4),
)


def digit(n, digits, bits):
    words = [
        sum(d << (bits * i) for i, d in enumerate(digits[s : s + 7])) for s in range(0, len(digits), 7)
    ]
    word, place = words[0], n
    for i in range(1, len(words)):
        word = jnp.where(n < 7 * i, word, words[i])
        place = jnp.where(n < 7 * i, place, n - 7 * i)
    return (word >> (bits * place)) & ((1 << bits) - 1)


def body(slabs, blocks, *refs):
    (
        start_hbm, velocity_hbm, source_hbm, time_ref, modulus_hbm, mass_hbm, crust_hbm,
        end_ref, hessian_ref,
        nat_u, nat_v, nat_s, nat_g, nat_m, nat_c,
        u, w, sf, im, hs, gx, gy, gz, uy, gy4, gz4, kx, kdx, kz, kdz, ub, pb, fs, fy,
        zs, zh, gzs, gzh, layer, crust, sent, got, index,
        in_sem, end_sem, zsend, zrecv, gzsend, gzrecv, gsend, grecv,
        usend, urecv, psend, precv, qsend, qrecv, hsend, hrecv, ready,
    ) = refs
    block = lax.axis_index("block")
    slab = lax.axis_index("slab")
    event = lax.axis_index("event")
    before = (lax.rem(block + blocks - 1, blocks), slab, event)
    after = (lax.rem(block + 1, blocks), slab, event)
    other_slab = (block, 1 - slab, event)
    other_event = (block, slab, 1 - event)

    plane = 8
    late = lax.rem(block, plane) == 0
    last = lax.rem(block, plane) == plane - 1
    barrier = pltpu.get_barrier_semaphore()
    for device in (before, other_slab, other_event):
        pl.semaphore_signal(barrier, inc=1, device_id=device, device_id_type=MESH)

    @pl.when(jnp.logical_not(last))
    def _():
        pl.semaphore_signal(barrier, inc=1, device_id=after, device_id_type=MESH)

    groups = ((0, 1), (7, 1), (1, 6))

    def start_early(group):
        first, count = groups[group]
        at = pl.ds(4 * first, 4 * count)
        for k in range(4):
            lanes = (slice(None), pl.ds(128 * k, 128))
            pairs = [(modulus_hbm.at[at, *lanes], nat_g.at[k, at], 0)]
            for e in range(2):
                pairs.append((start_hbm.at[e, at, *lanes], nat_u.at[k, at, e], 1))
            for source, target, kind in pairs:
                pltpu.make_async_copy(source, target, in_sem.at[kind, group]).start()

    def wait_early(group):
        first, count = groups[group]
        for kind, ref in enumerate((nat_g, nat_u)):
            part = ref.at[:, pl.ds(4 * first, 4 * count)]
            pltpu.make_async_copy(part, part, in_sem.at[kind, group]).wait()

    def start_late():
        for k in range(4):
            lanes = (slice(None), slice(None), pl.ds(128 * k, 128))
            pairs = [(mass_hbm.at[*lanes], nat_m.at[k], 0)]
            for e in range(2):
                pairs.append((source_hbm.at[e, *lanes], nat_s.at[k, :, e], 1))
                pairs.append((velocity_hbm.at[e, *lanes], nat_v.at[k, :, e], 2))
            for source, target, kind in pairs:
                pltpu.make_async_copy(source, target, in_sem.at[2, kind]).start()

    def wait_late():
        for kind, ref in enumerate((nat_m, nat_s, nat_v)):
            pltpu.make_async_copy(ref, ref, in_sem.at[2, kind]).wait()

    crust_load = pltpu.make_async_copy(crust_hbm, nat_c, gsend)
    crust_load.start()

    for group in range(3):
        start_early(group)
    start_late()

    lane = lax.broadcasted_iota(jnp.int32, TILE, 1)
    row = lax.broadcasted_iota(jnp.int32, TILE, 0)
    radial = row & 3
    for r in range(4):
        index[r] = 4 * (lane & 31) + ((r - (lane >> 5)) & 3)
        index[4 + r] = 32 * ((r - (lane & 3)) & 3) + (lane >> 2)
    bit0, bit1 = (lane & 1) == 1, (lane & 2) == 2
    block0, block1 = (lane & 32) == 32, (lane & 64) == 64
    upper = row < 4
    is0 = jnp.where(slab == 0, 1.0, 0.0).astype(jnp.float32)
    is1 = 1.0 - is0

    def gather(value, k):
        return jnp.take_along_axis(value, index[k], axis=1)

    def apart(t):
        x = [jnp.where(bit0, t[(r + 3) % 4], t[r]) for r in range(4)]
        m = [jnp.where(bit1, x[(r + 2) % 4], x[r]) for r in range(4)]
        n = [gather(m[r], r) for r in range(4)]
        y = [jnp.where(block0, n[(k + 1) % 4], n[k]) for k in range(4)]
        return [jnp.where(block1, y[(k + 2) % 4], y[k]) for k in range(4)]

    def together(o):
        y = [jnp.where(block0, o[(r + 3) % 4], o[r]) for r in range(4)]
        n = [jnp.where(block1, y[(r + 2) % 4], y[r]) for r in range(4)]
        m = [gather(n[r], 4 + r) for r in range(4)]
        z = [jnp.where(bit0, m[(k + 1) % 4], m[k]) for k in range(4)]
        return [jnp.where(bit1, z[(k + 2) % 4], z[k]) for k in range(4)]

    def turn(value, shift):
        return value if shift % 8 == 0 else pltpu.roll(value, shift % 8, 0)

    def pack(values, at):
        result = turn(values[0], -at)
        for k in range(1, 4):
            result = jnp.where(radial == k, turn(values[k], k - at), result)
        return result

    def next_lane(value):
        return jnp.where(lane == 127, 0.0, pltpu.roll(value, 127, 1))

    def lane_before(value):
        return jnp.where(lane == 0, 0.0, pltpu.roll(value, 1, 1))

    def twice_events(value):
        other = pltpu.roll(value, 4, 0)
        return jnp.where(upper, value, other), jnp.where(upper, other, value)

    def rows_of(ref, per):
        return ref.reshape(4 * 32 * per, 128)

    rows_u, rows_v, rows_s = rows_of(nat_u, 32), rows_of(nat_v, 32), rows_of(nat_s, 32)
    rows_g, rows_m, rows_sent = rows_of(nat_g, 16), rows_of(nat_m, 16), rows_of(sent, 16)

    def strided(ref, first, count):
        return [ref[pl.ds(first + count * k, 8, stride=4), :] for k in range(4)]

    edge_z = jnp.where(slab == 0, jnp.where(radial == 0, 0.1, 0.2), 0.2).astype(jnp.float32)
    edge_y = jnp.where(lane == 0, 0.1, 0.2).astype(jnp.float32)

    def over_z(value, zm):
        return value * (edge_z if zm == 0 else ASSEMBLED[zm])

    def over_y(value, ym):
        return value * (edge_y if ym == 0 else ASSEMBLED[ym])

    crust_load.wait()

    @pl.loop(0, 4)
    def _(part):
        at = pl.ds(pl.multiple_of(8 * part, 8), 8)
        found = apart([nat_c[at, pl.ds(128 * k, 128)] for k in range(4)])
        for k in range(4):
            crust[k, at, :] = found[k]

    def set_up(j):
        gxj, gyj, gzj = gx.at[j], gy.at[j], gz.at[j]
        for half in range(2):
            for zm in range(4):
                moduli = apart(strided(rows_g, 16 * (4 * j + 2 * half) + zm, 512))
                for ym in range(4):
                    fs[half, 4 * zm + ym] = moduli[ym]
        uj, ubj, uyj = u.at[j], ub.at[0, j], uy.at[j]
        for xm in range(4):
            x = 4 * j + xm
            for zm in range(4):
                values = apart(strided(rows_u, 32 * x + zm, 1024))
                for ym in range(4):
                    uj[xm, 4 * zm + ym] = values[ym]
                    if xm == 0:
                        ubj[4 * zm + ym] = values[ym]
        for half in range(2):
            x = 4 * j + 2 * half
            depth = [
                jnp.where(
                    upper,
                    jnp.broadcast_to(crust[ym, pl.ds(x, 1), :], TILE),
                    jnp.broadcast_to(crust[ym, pl.ds(x + 1, 1), :], TILE),
                )
                for ym in range(4)
            ]
            for zm in range(4):
                moduli = [fs[half, 4 * zm + ym] for ym in range(4)]
                place = slab * 16 + 4 * radial + zm
                for ym in range(4):
                    stiff = jnp.where(
                        place >= 16 * slabs - depth[ym], CRUST_FACTOR * moduli[ym], moduli[ym]
                    )
                    at = 4 * zm + ym
                    for side, value in enumerate(twice_events(stiff)):
                        xm = 2 * half + side
                        in_y, in_z = over_y(value, ym), over_z(value, zm)
                        gxj[xm, at] = over_z(in_y, zm) * RHO[xm]
                        gyj[xm, at] = in_z * (RHO[ym] * ASSEMBLED[xm])
                        gzj[xm, at] = in_y * (RHO[zm] * ASSEMBLED[xm])
        for half in range(2):
            for zm in range(4):
                gy4[j, 2 * half, zm] = next_lane(gyj[2 * half, 4 * zm])
                gy4[j, 2 * half + 1, zm] = next_lane(gyj[2 * half + 1, 4 * zm])
        for xm in range(4):
            for zm in range(4):
                uyj[xm, zm] = next_lane(uj[xm, 4 * zm])
        for xm in range(4):
            first = pack([gzj[xm, ym] for ym in range(4)], 0)
            ends = [pack([gzj[xm, 4 * zm + ym] for ym in range(4)], 3) for zm in range(4)]
            for zm in range(4):
                kz[j, xm, zm] = ends[zm]
            total = sum(ends[zm] * float(DN[zm, 4] ** 2) for zm in range(4))
            gzs[j, xm] = is0 * total + is1 * first

    def gz_copy(j, count=1):
        at = pl.ds(j, count)
        return pltpu.make_async_remote_copy(
            src_ref=gzs.at[at], dst_ref=gzh.at[at], send_sem=gzsend, recv_sem=gzrecv,
            device_id=other_slab, device_id_type=MESH,
        )

    def z_copy(t, j):
        return pltpu.make_async_remote_copy(
            src_ref=zs.at[t, j], dst_ref=zh.at[t, j], send_sem=zsend, recv_sem=zrecv.at[t, j],
            device_id=other_slab, device_id_type=MESH,
        )

    def u_copy(t):
        return pltpu.make_async_remote_copy(
            src_ref=ub.at[t, 0], dst_ref=ub.at[t, 8], send_sem=usend.at[t], recv_sem=urecv.at[t],
            device_id=before, device_id_type=MESH,
        )

    def g_copy():
        return pltpu.make_async_remote_copy(
            src_ref=gx.at[0, 0], dst_ref=gx.at[8, 0], send_sem=gsend, recv_sem=grecv,
            device_id=before, device_id_type=MESH,
        )

    def p_copy(t):
        return pltpu.make_async_remote_copy(
            src_ref=pb.at[t, 8], dst_ref=pb.at[t, 0], send_sem=psend.at[t], recv_sem=precv.at[t],
            device_id=after, device_id_type=MESH,
        )

    def layer_copy():
        return pltpu.make_async_remote_copy(
            src_ref=layer.at[pl.ds(0, 3)], dst_ref=layer.at[pl.ds(3, 3)], send_sem=qsend, recv_sem=qrecv,
            device_id=after, device_id_type=MESH,
        )

    def h_copy(j):
        at = pl.ds(4 * j, 4)
        return pltpu.make_async_remote_copy(
            src_ref=sent.at[:, at], dst_ref=got.at[:, at], send_sem=hsend.at[j], recv_sem=hrecv.at[j],
            device_id=other_event, device_id_type=MESH,
        )

    @pl.loop(0, 8)
    def _(n):
        j = lax.rem(7 * n, 8)
        for group in range(3):

            @pl.when(n == group)
            def _():
                wait_early(group)

        set_up(j)

        @pl.when(n == 0)
        def _():
            @pl.when(late)
            def _():
                pl.semaphore_wait(barrier, 3)

            @pl.when(jnp.logical_not(late))
            def _():
                pl.semaphore_wait(barrier, 4)
                u_copy(0).start()
                g_copy().start()

            @pl.when(last)
            def _():
                pl.semaphore_signal(ready, inc=1, device_id=after, device_id_type=MESH)

        gz_copy(j).start()

        @pl.when(n == 1)
        def _():
            for k in range(16):
                g = [gx[7, i, k] for i in range(4)]
                v = [u[7, i, k] for i in range(4)]
                scaled = [g[i] * float(DN[i, 4]) for i in range(4)]
                layer[2, k] = sum(scaled[i] * float(DN[i, 4]) for i in range(4))
                layer[0, k] = sum(
                    scaled[i] * sum(float(DN[i, m]) * v[m] for m in range(4)) for i in range(4)
                )
                layer[1, k] = sum(float(DN[4, m]) * v[m] for m in range(4))
            layer_copy().start()

    def next_coefs(j):
        gj, gn, kj, kn = gx.at[j], gx.at[j + 1, 0], kx.at[j], kdx.at[j + 1]
        for k in range(16):
            scaled = [gj[i, k] * float(DN[i, 4]) for i in range(4)] + [gn[k] * float(DN[4, 4])]
            for m in range(4):
                kj[m, k] = sum(scaled[i] * float(DN[i, m]) for i in range(5))
            kn[k] = sum(scaled[i] * float(DN[i, 4]) for i in range(5))

    def partial_x(t, j):
        uj, kj, pj = u.at[j], kx.at[j], pb.at[t, j + 1]
        for k in range(16):
            pj[k] = (kj[0, k] * uj[0, k] + kj[1, k] * uj[1, k]) + (
                kj[2, k] * uj[2, k] + kj[3, k] * uj[3, k]
            )

    @pl.loop(0, 7)
    def _(j):
        next_coefs(j)
        partial_x(0, j)

    def send_z(t, j):
        uj, zj = u.at[j], zs.at[t, j]

        @pl.when(slab == 0)
        def _():
            kj = kz.at[j]
            for xm in range(4):
                packed = [pack([uj[xm, 4 * zm + ym] for ym in range(4)], 3) for zm in range(4)]
                zj[xm] = (kj[xm, 0] * packed[0] + kj[xm, 1] * packed[1]) + (
                    kj[xm, 2] * packed[2] + kj[xm, 3] * packed[3]
                )

        @pl.when(slab != 0)
        def _():
            for xm in range(4):
                zj[xm] = pack([uj[xm, ym] for ym in range(4)], 0)

        z_copy(t, j).start()

    gz_copy(0, 8).wait_recv()

    @pl.loop(0, 8)
    def _(n):
        j = lax.rem(n + 1, 8)
        gzj, gz4j, kzj, kdzj, gzhj = gz.at[j], gz4.at[j], kz.at[j], kdz.at[j], gzh.at[j]
        for xm in range(4):
            arrived = gzhj[xm]
            above, below = arrived * is0, arrived * is1
            for ym in range(4):
                own = gzj[xm, ym]
                gz4j[xm, ym] = jnp.where(radial == 3, turn(above, 3 - ym), turn(own, 7))
                diagonal = turn(below, -ym) + is1 * float(DN[4, 4] ** 2) * own
                kdzj[xm, ym] = jnp.where(radial == 0, diagonal, 0.0)
            ends = [kzj[xm, zm] for zm in range(4)] + [arrived]
            scaled = [ends[i] * float(DN[i, 4]) for i in range(5)]
            for m in range(4):
                kzj[xm, m] = sum(scaled[i] * float(DN[i, m]) for i in range(5))
        send_z(0, j)

    def advance(j, t, first):
        z_copy(t - 1, j).wait_recv()
        uj, gxj, gyj, gzj, uyj = u.at[j], gx.at[j], gy.at[j], gz.at[j], uy.at[j]
        gy4j, gz4j, kdzj, zhj = gy4.at[j], gz4.at[j], kdz.at[j], zh.at[t - 1, j]
        imj, sfj, wj, hsj = im.at[j], sf.at[j], w.at[j], hs.at[j]

        for xm in range(4):
            x = 4 * j + xm
            if first:
                for zm in range(4):
                    if xm % 2 == 0:
                        masses = apart(strided(rows_m, 16 * x + zm, 512))
                        for ym in range(4):
                            mass = masses[ym] * (TIME_STEP * TIME_STEP)
                            one, two = twice_events(mass)
                            imj[xm, 4 * zm + ym], imj[xm + 1, 4 * zm + ym] = one, two
                    values = apart(strided(rows_v, 32 * x + zm, 1024))
                    for ym in range(4):
                        wj[xm, 4 * zm + ym] = values[ym] * TIME_STEP
                    values = apart(strided(rows_s, 32 * x + zm, 1024))
                    for ym in range(4):
                        sfj[xm, 4 * zm + ym] = values[ym] * imj[xm, 4 * zm + ym]
            v = [[uj[xm, 4 * zm + ym] for ym in range(4)] for zm in range(4)]
            f = [[None] * 4 for _ in range(4)]
            arrived = zhj[xm]
            above, below = arrived * is0, arrived * is1
            for ym in range(4):
                u4 = jnp.where(radial == 3, turn(above, 3 - ym), turn(v[0][ym], 7))
                parts = line(
                    *[v[zm][ym] for zm in range(4)], u4,
                    *[gzj[xm, 4 * zm + ym] for zm in range(4)], gz4j[xm, ym],
                )
                carried = jnp.where(radial == 0, turn(below, -ym), turn(parts[4], 1))
                f[0][ym] = (parts[0] + carried) + kdzj[xm, ym] * v[0][ym]
                f[1][ym], f[3][ym] = parts[1], parts[3]
                f[2][ym] = -parts[2]
            for zm in range(4):
                parts = line(
                    *v[zm], uyj[xm, zm], *[gyj[xm, 4 * zm + ym] for ym in range(4)], gy4j[xm, zm]
                )
                fy[xm, zm] = parts[4]
                fs[xm, 4 * zm] = f[zm][0] + parts[0]
                fs[xm, 4 * zm + 1] = f[zm][1] + parts[1]
                fs[xm, 4 * zm + 2] = f[zm][2] - parts[2]
                fs[xm, 4 * zm + 3] = f[zm][3] + parts[3]

        for xm in range(4):
            for zm in range(4):
                fy[xm, zm] = lane_before(fy[xm, zm])

        strength = jnp.where(upper, time_ref[0, t - 1], time_ref[1, t - 1])
        ubn, pbj, kdxj, gxn = ub.at[t - 1, j + 1], pb.at[t - 1, j], kdx.at[j], gx.at[j + 1, 0]
        for k in range(16):
            v = [uj[i, k] for i in range(4)]
            parts = line(*v, ubn[k], *[gxj[i, k] for i in range(4)], gxn[k], last=False)
            f = [
                fs[0, k] + (parts[0] + (pbj[k] + kdxj[k] * v[0])),
                fs[1, k] + parts[1],
                fs[2, k] - parts[2],
                fs[3, k] + parts[3],
            ]
            for i in range(4):
                if k % 4 == 0:
                    f[i] = f[i] + fy[i, k // 4]
                kick = strength * sfj[i, k] - imj[i, k] * f[i]
                speed = wj[i, k] + kick
                wj[i, k] = speed
                moved = v[i] + speed
                uj[i, k] = moved
                hsj[i, k] = kick * kick if first else hsj[i, k] + kick * kick
                if k % 4 == 0:
                    uyj[i, k // 4] = next_lane(moved)

    def hand_on(j, t):
        send_z(t, j)
        uj, ubj = u.at[j], ub.at[t, j]
        for k in range(16):
            ubj[k] = uj[0, k]
        partial_x(t, j)

        @pl.when(j == 0)
        def _():
            u_copy(t).start()

        @pl.when(j == 7)
        def _():
            p_copy(t).start()

    def end_copy(j, k, e):
        at = pl.ds(4 * j, 4)
        return pltpu.make_async_copy(
            nat_u.at[k, at, e], end_ref.at[e, at, :, pl.ds(128 * k, 128)], end_sem
        )

    def finish(j):
        uj, hsj = u.at[j], hs.at[j]
        for half in range(2):
            for zm in range(4):
                for ym in range(4):
                    one, two = hsj[2 * half, 4 * zm + ym], hsj[2 * half + 1, 4 * zm + ym]
                    one = one + pltpu.roll(one, 4, 0)
                    two = two + pltpu.roll(two, 4, 0)
                    fs[half, 4 * zm + ym] = jnp.where(upper, one, two) * (100.0 / (4 * STEPS))
        for half in range(2):
            for zm in range(4):
                both = [fs[half, 4 * zm + ym] for ym in range(4)]
                for k, value in enumerate(together(both)):
                    first = 512 * k + 16 * (4 * j + 2 * half) + zm
                    rows_sent[pl.ds(first, 8, stride=4), :] = value
        h_copy(j).start()
        for xm in range(4):
            for zm in range(4):
                whole = together([uj[xm, 4 * zm + ym] for ym in range(4)])
                for k, value in enumerate(whole):
                    rows_u[pl.ds(1024 * k + 32 * (4 * j + xm) + zm, 8, stride=4), :] = value
        for k in range(4):
            for e in range(2):
                end_copy(j, k, e).start()

    wait_late()

    @pl.loop(0, len(ORDER))
    def _(n):
        j, t = [
            jnp.where(block == 0, digit(n, [task[i] for task in ORDER_OF_FIRST], 4), digit(n, [task[i] for task in ORDER], 4))
            for i in range(2)
        ]

        @pl.when(jnp.logical_and(late, n == jnp.where(block == 0, 4, 0)))
        def _():
            pl.semaphore_wait(ready, 1)
            u_copy(0).start()
            g_copy().start()

        @pl.when(t == 1)
        def _():
            @pl.when(j == 0)
            def _():
                layer_copy().wait_recv()
                for k in range(16):
                    own = gx[0, 0, k] * float(DN[4, 4])
                    pb[0, 0, k] = layer[3, k] + own * layer[4, k]
                    kdx[0, k] = layer[5, k] + own * float(DN[4, 4])

            @pl.when(j == 7)
            def _():
                u_copy(0).wait_recv()
                g_copy().wait_recv()
                next_coefs(7)

            advance(j, t, True)
            hand_on(j, t)

        @pl.when(t > 1)
        def _():
            @pl.when(j == 0)
            def _():
                p_copy(t - 1).wait_recv()

            @pl.when(j == 7)
            def _():
                u_copy(t - 1).wait_recv()

            advance(j, t, False)

            @pl.when(t < STEPS)
            def _():
                hand_on(j, t)

            @pl.when(t == STEPS)
            def _():
                finish(j)

    @pl.loop(0, 8)
    def _(n):
        j = jnp.where(
            block == 0, *[digit(n, [j for j, t in order if t == STEPS], 4) for order in (ORDER_OF_FIRST, ORDER)]
        )
        h_copy(j).wait_recv()
        for xm in range(4):
            x = 4 * j + xm
            for k in range(4):
                hessian_ref[x, :, pl.ds(128 * k, 128)] = sent[k, x] + got[k, x]

    u_copy(0).wait_send()
    g_copy().wait_send()
    layer_copy().wait_send()
    gz_copy(0, 8).wait_send()
    for t in range(1, 4):
        u_copy(t).wait_send()
        p_copy(t).wait_send()

    @pl.loop(0, 8)
    def _(j):
        h_copy(j).wait_send()

    pltpu.make_async_copy(zs, zs, zsend).wait()
    pltpu.make_async_copy(nat_u, nat_u, end_sem).wait()


def per_device(slabs, blocks, *arrays):
    anywhere = pl.BlockSpec(memory_space=pl.ANY)
    inside = pl.BlockSpec(memory_space=pltpu.VMEM)

    def tiles(*shape):
        return pltpu.VMEM((*shape, 8, 128), jnp.float32)

    field, natural = tiles(8, 4, 16), pltpu.VMEM((4, 32, 16, 128), jnp.float32)
    natural_events = pltpu.VMEM((4, 32, 2, 16, 128), jnp.float32)
    several = pltpu.SemaphoreType.DMA
    scratch = [
        natural_events, natural_events, natural_events,
        natural, natural, pltpu.VMEM((32, 512), jnp.int32),
        field, field, field, field, field,
        tiles(9, 4, 16), field, field,
        tiles(8, 4, 4), tiles(8, 4, 4), tiles(8, 4, 4),
        tiles(8, 4, 16), tiles(9, 16), tiles(8, 4, 4), tiles(8, 4, 4),
        tiles(4, 9, 16), tiles(4, 9, 16), tiles(4, 16), tiles(4, 4),
        tiles(4, 8, 4), tiles(4, 8, 4), tiles(8, 4), tiles(8, 4),
        tiles(6, 16), pltpu.VMEM((4, 32, 128), jnp.int32),
        natural, natural, pltpu.VMEM((8, 8, 128), jnp.int32),
        several((3, 3)), several, several, several((4, 8)),
        several, several, several, several,
        several((4,)), several((4,)), several((4,)), several((4,)),
        several, several, several((8,)), several((8,)),
        pltpu.SemaphoreType.REGULAR,
    ]
    return pl.pallas_call(
        functools.partial(body, slabs, blocks),
        out_shape=(
            pltpu.VMEM((2, 32, 16, 512), jnp.float32),
            pltpu.VMEM((32, 16, 512), jnp.float32),
        ),
        in_specs=[anywhere] * 3 + [pl.BlockSpec(memory_space=pltpu.SMEM)] + [anywhere] * 3,
        out_specs=(inside, inside),
        scratch_shapes=scratch,
        compiler_params=pltpu.CompilerParams(
            collective_id=0, has_side_effects=True, vmem_limit_bytes=56 << 20
        ),
        name="adjoint_steps",
    )(*arrays)


def solution(mesh):
    in_specs = (
        P("event", "block", "slab", None),
        P("event", "block", "slab", None),
        P("event", "block", "slab", None),
        P("event", None),
        P("block", "slab", None),
        P("block", "slab", None),
        P("block", None),
    )
    out_specs = (P("event", "block", "slab", None), P("block", "slab", None))
    return jax.shard_map(
        functools.partial(per_device, mesh.shape["slab"], mesh.shape["block"]),
        mesh=mesh, in_specs=in_specs, out_specs=out_specs, check_vma=False,
    )
```

```python
import functools

import jax
import jax.numpy as jnp
import numpy as np
from jax import lax
from jax.experimental import pallas as pl
from jax.experimental.pallas import tpu as pltpu
from jax.sharding import PartitionSpec as P

STEPS = 4
TIME_STEP = 0.1
CRUST_FACTOR = 0.35
WEIGHTS = (0.1, 49.0 / 90.0, 32.0 / 45.0, 49.0 / 90.0, 0.1)
ASSEMBLED = (0.2, 49.0 / 90.0, 32.0 / 45.0, 49.0 / 90.0)
MESH = pl.DeviceIdType.MESH
TILE = (8, 128)


def derivative_table():
    points = np.array([-1.0, -np.sqrt(3.0 / 7.0), 0.0, np.sqrt(3.0 / 7.0), 1.0])
    scales = np.array(
        [
            np.prod([points[one] - points[other] for other in range(5) if other != one])
            for one in range(5)
        ]
    )
    table = np.zeros((5, 5))
    for target in range(5):
        for anchor in range(5):
            if target != anchor:
                table[target, anchor] = scales[target] / (
                    scales[anchor] * (points[target] - points[anchor])
                )
        table[target, target] = -np.sum(table[target])
    return table


D = derivative_table()
A4, B4 = (D[4, 4] - D[4, 0]) / 2, (D[4, 3] - D[4, 1]) / 2
E4, T4 = (D[4, 4] + D[4, 0]) / 2, (D[4, 3] + D[4, 1]) / 2
A3, B3 = (D[3, 4] - D[3, 0]) / 2, (D[3, 3] - D[3, 1]) / 2
E3, T3 = (D[3, 4] + D[3, 0]) / 2, (D[3, 3] + D[3, 1]) / 2
SCALE = (A4, A3, D[2, 3], A3, A4)
DN = D / np.array(SCALE)[:, None]
KAPPA0, GAMMA, DELTA = B4 / A4, E4 / A4, T4 / A4
KAPPA1, EPSILON, ZETA = B3 / A3, E3 / A3, T3 / A3
KAPPA2 = D[2, 4] / D[2, 3]
RHO = [WEIGHTS[i] * SCALE[i] ** 2 for i in range(5)]


def line(u0, u1, u2, u3, u4, c0, c1, c2, c3, c4, last=True):
    a, b = u4 - u0, u3 - u1
    twice = u2 + u2
    e, f = (u4 + u0) - twice, (u3 + u1) - twice
    p, q = a + KAPPA0 * b, GAMMA * e + DELTA * f
    r, s = a + KAPPA1 * b, EPSILON * e + ZETA * f
    h4, h0 = (p + q) * c4, (p - q) * c0
    h3, h1 = (r + s) * c3, (r - s) * c1
    h2 = (b + KAPPA2 * a) * c2
    hp, hm = h4 + h0, h4 - h0
    ep, em = h3 + h1, h3 - h1
    fa = (hp + ep) + KAPPA2 * h2
    fb = (KAPPA0 * hp + KAPPA1 * ep) + h2
    fe = GAMMA * hm + EPSILON * em
    ff = DELTA * hm + ZETA * em
    total = fe + ff
    return fe - fa, ff - fb, total + total, ff + fb, (fe + fa if last else None)


ORDER = (
    (4, 1), (3, 1), (2, 1), (1, 1), (7, 1), (2, 2), (0, 1), (6, 1), (5, 1), (3, 2), (4, 2), (1, 2),
    (2, 3), (0, 2), (1, 3), (7, 2), (3, 3), (2, 4), (5, 2), (6, 2), (4, 3), (3, 4), (6, 3), (0, 3),
    (5, 3), (1, 4), (7, 3), (5, 4), (4, 4), (6, 4), (0, 4), (7, 4),
)
ORDER_OF_FIRST = (
    (4, 1), (3, 1), (5, 1), (2, 1), (6, 1), (1, 1), (3, 2), (4, 2), (5, 2), (2, 2), (4, 3), (3, 3),
    (7, 1), (6, 2), (5, 3), (4, 4), (0, 1), (1, 2), (2, 3), (3, 4), (7, 2), (6, 3), (5, 4), (0, 2),
    (1, 3), (2, 4), (7, 3), (6, 4), (0, 3), (1, 4), (7, 4), (0, 4),
)


def digit(n, digits, bits):
    words = [
        sum(d << (bits * i) for i, d in enumerate(digits[s : s + 7])) for s in range(0, len(digits), 7)
    ]
    word, place = words[0], n
    for i in range(1, len(words)):
        word = jnp.where(n < 7 * i, word, words[i])
        place = jnp.where(n < 7 * i, place, n - 7 * i)
    return (word >> (bits * place)) & ((1 << bits) - 1)


def place_out(end_in, hessian_in, end_out, hessian_out, sem):
    half = [pl.ds(0, 16), pl.ds(16, 16)]
    pairs = [(end_in.at[e, at], end_out.at[e, at]) for e in range(2) for at in half]
    pairs += [(hessian_in.at[at], hessian_out.at[at]) for at in half]
    copies = [pltpu.make_async_copy(*pair, sem.at[i]) for i, pair in enumerate(pairs)]
    for copy in copies:
        copy.start()
    for copy in copies:
        copy.wait()


def body(slabs, blocks, *refs):
    (
        start_hbm, velocity_hbm, source_hbm, time_ref, modulus_hbm, mass_hbm, crust_hbm,
        end_ref, hessian_ref,
        nat_u, nat_v, nat_s, nat_g, nat_m, nat_c,
        u, w, sf, im, hs, gx, gy, gz, uy, gy4, gz4, kx, kdx, kz, kdz, ub, pb, fs, fy,
        zs, zh, gzs, gzh, layer, crust, sent, got, index,
        in_sem, end_sem, zsend, zrecv, gzsend, gzrecv, gsend, grecv,
        usend, urecv, psend, precv, qsend, qrecv, hsend, hrecv, ready,
    ) = refs
    block = lax.axis_index("block")
    slab = lax.axis_index("slab")
    event = lax.axis_index("event")
    before = (lax.rem(block + blocks - 1, blocks), slab, event)
    after = (lax.rem(block + 1, blocks), slab, event)
    other_slab = (block, 1 - slab, event)
    other_event = (block, slab, 1 - event)

    plane = 8
    late = lax.rem(block, plane) == 0
    last = lax.rem(block, plane) == plane - 1
    barrier = pltpu.get_barrier_semaphore()
    for device in (before, other_slab, other_event):
        pl.semaphore_signal(barrier, inc=1, device_id=device, device_id_type=MESH)

    @pl.when(jnp.logical_not(last))
    def _():
        pl.semaphore_signal(barrier, inc=1, device_id=after, device_id_type=MESH)

    groups = ((0, 1), (7, 1), (1, 6))

    def start_early(group):
        first, count = groups[group]
        at = pl.ds(4 * first, 4 * count)
        for k in range(4):
            lanes = (slice(None), pl.ds(128 * k, 128))
            pairs = [(modulus_hbm.at[at, *lanes], nat_g.at[k, at], 0)]
            for e in range(2):
                pairs.append((start_hbm.at[e, at, *lanes], nat_u.at[k, at, e], 1))
            for source, target, kind in pairs:
                pltpu.make_async_copy(source, target, in_sem.at[kind, group]).start()

    def wait_early(group):
        first, count = groups[group]
        for kind, ref in enumerate((nat_g, nat_u)):
            part = ref.at[:, pl.ds(4 * first, 4 * count)]
            pltpu.make_async_copy(part, part, in_sem.at[kind, group]).wait()

    def start_late():
        for k in range(4):
            lanes = (slice(None), slice(None), pl.ds(128 * k, 128))
            pairs = [(mass_hbm.at[*lanes], nat_m.at[k], 0)]
            for e in range(2):
                pairs.append((source_hbm.at[e, *lanes], nat_s.at[k, :, e], 1))
                pairs.append((velocity_hbm.at[e, *lanes], nat_v.at[k, :, e], 2))
            for source, target, kind in pairs:
                pltpu.make_async_copy(source, target, in_sem.at[2, kind]).start()

    def wait_late():
        for kind, ref in enumerate((nat_m, nat_s, nat_v)):
            pltpu.make_async_copy(ref, ref, in_sem.at[2, kind]).wait()

    crust_load = pltpu.make_async_copy(crust_hbm, nat_c, gsend)
    crust_load.start()

    for group in range(3):
        start_early(group)
    start_late()

    lane = lax.broadcasted_iota(jnp.int32, TILE, 1)
    row = lax.broadcasted_iota(jnp.int32, TILE, 0)
    radial = row & 3
    for r in range(4):
        index[r] = 4 * (lane & 31) + ((r - (lane >> 5)) & 3)
        index[4 + r] = 32 * ((r - (lane & 3)) & 3) + (lane >> 2)
    bit0, bit1 = (lane & 1) == 1, (lane & 2) == 2
    block0, block1 = (lane & 32) == 32, (lane & 64) == 64
    upper = row < 4
    is0 = jnp.where(slab == 0, 1.0, 0.0).astype(jnp.float32)
    is1 = 1.0 - is0

    def gather(value, k):
        return jnp.take_along_axis(value, index[k], axis=1)

    def apart(t):
        x = [jnp.where(bit0, t[(r + 3) % 4], t[r]) for r in range(4)]
        m = [jnp.where(bit1, x[(r + 2) % 4], x[r]) for r in range(4)]
        n = [gather(m[r], r) for r in range(4)]
        y = [jnp.where(block0, n[(k + 1) % 4], n[k]) for k in range(4)]
        return [jnp.where(block1, y[(k + 2) % 4], y[k]) for k in range(4)]

    def together(o):
        y = [jnp.where(block0, o[(r + 3) % 4], o[r]) for r in range(4)]
        n = [jnp.where(block1, y[(r + 2) % 4], y[r]) for r in range(4)]
        m = [gather(n[r], 4 + r) for r in range(4)]
        z = [jnp.where(bit0, m[(k + 1) % 4], m[k]) for k in range(4)]
        return [jnp.where(bit1, z[(k + 2) % 4], z[k]) for k in range(4)]

    def turn(value, shift):
        return value if shift % 8 == 0 else pltpu.roll(value, shift % 8, 0)

    def pack(values, at):
        result = turn(values[0], -at)
        for k in range(1, 4):
            result = jnp.where(radial == k, turn(values[k], k - at), result)
        return result

    def next_lane(value):
        return jnp.where(lane == 127, 0.0, pltpu.roll(value, 127, 1))

    def lane_before(value):
        return jnp.where(lane == 0, 0.0, pltpu.roll(value, 1, 1))

    def twice_events(value):
        other = pltpu.roll(value, 4, 0)
        return jnp.where(upper, value, other), jnp.where(upper, other, value)

    def rows_of(ref, per):
        return ref.reshape(4 * 32 * per, 128)

    rows_u, rows_v, rows_s = rows_of(nat_u, 32), rows_of(nat_v, 32), rows_of(nat_s, 32)
    rows_g, rows_m, rows_sent = rows_of(nat_g, 16), rows_of(nat_m, 16), rows_of(sent, 16)

    def strided(ref, first, count):
        return [ref[pl.ds(first + count * k, 8, stride=4), :] for k in range(4)]

    edge_z = jnp.where(slab == 0, jnp.where(radial == 0, 0.1, 0.2), 0.2).astype(jnp.float32)
    edge_y = jnp.where(lane == 0, 0.1, 0.2).astype(jnp.float32)

    def over_z(value, zm):
        return value * (edge_z if zm == 0 else ASSEMBLED[zm])

    def over_y(value, ym):
        return value * (edge_y if ym == 0 else ASSEMBLED[ym])

    crust_load.wait()

    @pl.loop(0, 4)
    def _(part):
        at = pl.ds(pl.multiple_of(8 * part, 8), 8)
        found = apart([nat_c[at, pl.ds(128 * k, 128)] for k in range(4)])
        for k in range(4):
            crust[k, at, :] = found[k]

    def set_up(j):
        gxj, gyj, gzj = gx.at[j], gy.at[j], gz.at[j]
        for half in range(2):
            for zm in range(4):
                moduli = apart(strided(rows_g, 16 * (4 * j + 2 * half) + zm, 512))
                for ym in range(4):
                    fs[half, 4 * zm + ym] = moduli[ym]
        uj, ubj, uyj = u.at[j], ub.at[0, j], uy.at[j]
        for xm in range(4):
            x = 4 * j + xm
            for zm in range(4):
                values = apart(strided(rows_u, 32 * x + zm, 1024))
                for ym in range(4):
                    uj[xm, 4 * zm + ym] = values[ym]
                    if xm == 0:
                        ubj[4 * zm + ym] = values[ym]
        for half in range(2):
            x = 4 * j + 2 * half
            depth = [
                jnp.where(
                    upper,
                    jnp.broadcast_to(crust[ym, pl.ds(x, 1), :], TILE),
                    jnp.broadcast_to(crust[ym, pl.ds(x + 1, 1), :], TILE),
                )
                for ym in range(4)
            ]
            for zm in range(4):
                moduli = [fs[half, 4 * zm + ym] for ym in range(4)]
                place = slab * 16 + 4 * radial + zm
                for ym in range(4):
                    stiff = jnp.where(
                        place >= 16 * slabs - depth[ym], CRUST_FACTOR * moduli[ym], moduli[ym]
                    )
                    at = 4 * zm + ym
                    for side, value in enumerate(twice_events(stiff)):
                        xm = 2 * half + side
                        in_y, in_z = over_y(value, ym), over_z(value, zm)
                        gxj[xm, at] = over_z(in_y, zm) * RHO[xm]
                        gyj[xm, at] = in_z * (RHO[ym] * ASSEMBLED[xm])
                        gzj[xm, at] = in_y * (RHO[zm] * ASSEMBLED[xm])
        for half in range(2):
            for zm in range(4):
                gy4[j, 2 * half, zm] = next_lane(gyj[2 * half, 4 * zm])
                gy4[j, 2 * half + 1, zm] = next_lane(gyj[2 * half + 1, 4 * zm])
        for xm in range(4):
            for zm in range(4):
                uyj[xm, zm] = next_lane(uj[xm, 4 * zm])
        for xm in range(4):
            first = pack([gzj[xm, ym] for ym in range(4)], 0)
            ends = [pack([gzj[xm, 4 * zm + ym] for ym in range(4)], 3) for zm in range(4)]
            for zm in range(4):
                kz[j, xm, zm] = ends[zm]
            total = sum(ends[zm] * float(DN[zm, 4] ** 2) for zm in range(4))
            gzs[j, xm] = is0 * total + is1 * first

    def gz_copy(j, count=1):
        at = pl.ds(j, count)
        return pltpu.make_async_remote_copy(
            src_ref=gzs.at[at], dst_ref=gzh.at[at], send_sem=gzsend, recv_sem=gzrecv,
            device_id=other_slab, device_id_type=MESH,
        )

    def z_copy(t, j):
        return pltpu.make_async_remote_copy(
            src_ref=zs.at[t, j], dst_ref=zh.at[t, j], send_sem=zsend, recv_sem=zrecv.at[t, j],
            device_id=other_slab, device_id_type=MESH,
        )

    def u_copy(t):
        return pltpu.make_async_remote_copy(
            src_ref=ub.at[t, 0], dst_ref=ub.at[t, 8], send_sem=usend.at[t], recv_sem=urecv.at[t],
            device_id=before, device_id_type=MESH,
        )

    def g_copy():
        return pltpu.make_async_remote_copy(
            src_ref=gx.at[0, 0], dst_ref=gx.at[8, 0], send_sem=gsend, recv_sem=grecv,
            device_id=before, device_id_type=MESH,
        )

    def p_copy(t):
        return pltpu.make_async_remote_copy(
            src_ref=pb.at[t, 8], dst_ref=pb.at[t, 0], send_sem=psend.at[t], recv_sem=precv.at[t],
            device_id=after, device_id_type=MESH,
        )

    def layer_copy():
        return pltpu.make_async_remote_copy(
            src_ref=layer.at[pl.ds(0, 3)], dst_ref=layer.at[pl.ds(3, 3)], send_sem=qsend, recv_sem=qrecv,
            device_id=after, device_id_type=MESH,
        )

    def h_copy(j):
        at = pl.ds(4 * j, 4)
        return pltpu.make_async_remote_copy(
            src_ref=sent.at[:, at], dst_ref=got.at[:, at], send_sem=hsend.at[j], recv_sem=hrecv.at[j],
            device_id=other_event, device_id_type=MESH,
        )

    @pl.loop(0, 8)
    def _(n):
        j = lax.rem(7 * n, 8)
        for group in range(3):

            @pl.when(n == group)
            def _():
                wait_early(group)

        set_up(j)

        @pl.when(n == 0)
        def _():
            @pl.when(late)
            def _():
                pl.semaphore_wait(barrier, 3)

            @pl.when(jnp.logical_not(late))
            def _():
                pl.semaphore_wait(barrier, 4)
                u_copy(0).start()
                g_copy().start()

            @pl.when(last)
            def _():
                pl.semaphore_signal(ready, inc=1, device_id=after, device_id_type=MESH)

        gz_copy(j).start()

        @pl.when(n == 1)
        def _():
            for k in range(16):
                g = [gx[7, i, k] for i in range(4)]
                v = [u[7, i, k] for i in range(4)]
                scaled = [g[i] * float(DN[i, 4]) for i in range(4)]
                layer[2, k] = sum(scaled[i] * float(DN[i, 4]) for i in range(4))
                layer[0, k] = sum(
                    scaled[i] * sum(float(DN[i, m]) * v[m] for m in range(4)) for i in range(4)
                )
                layer[1, k] = sum(float(DN[4, m]) * v[m] for m in range(4))
            layer_copy().start()

    def next_coefs(j):
        gj, gn, kj, kn = gx.at[j], gx.at[j + 1, 0], kx.at[j], kdx.at[j + 1]
        for k in range(16):
            scaled = [gj[i, k] * float(DN[i, 4]) for i in range(4)] + [gn[k] * float(DN[4, 4])]
            for m in range(4):
                kj[m, k] = sum(scaled[i] * float(DN[i, m]) for i in range(5))
            kn[k] = sum(scaled[i] * float(DN[i, 4]) for i in range(5))

    def partial_x(t, j):
        uj, kj, pj = u.at[j], kx.at[j], pb.at[t, j + 1]
        for k in range(16):
            pj[k] = (kj[0, k] * uj[0, k] + kj[1, k] * uj[1, k]) + (
                kj[2, k] * uj[2, k] + kj[3, k] * uj[3, k]
            )

    @pl.loop(0, 7)
    def _(j):
        next_coefs(j)
        partial_x(0, j)

    def send_z(t, j):
        uj, zj = u.at[j], zs.at[t, j]

        @pl.when(slab == 0)
        def _():
            kj = kz.at[j]
            for xm in range(4):
                packed = [pack([uj[xm, 4 * zm + ym] for ym in range(4)], 3) for zm in range(4)]
                zj[xm] = (kj[xm, 0] * packed[0] + kj[xm, 1] * packed[1]) + (
                    kj[xm, 2] * packed[2] + kj[xm, 3] * packed[3]
                )

        @pl.when(slab != 0)
        def _():
            for xm in range(4):
                zj[xm] = pack([uj[xm, ym] for ym in range(4)], 0)

        z_copy(t, j).start()

    gz_copy(0, 8).wait_recv()

    @pl.loop(0, 8)
    def _(n):
        j = lax.rem(n + 1, 8)
        gzj, gz4j, kzj, kdzj, gzhj = gz.at[j], gz4.at[j], kz.at[j], kdz.at[j], gzh.at[j]
        for xm in range(4):
            arrived = gzhj[xm]
            above, below = arrived * is0, arrived * is1
            for ym in range(4):
                own = gzj[xm, ym]
                gz4j[xm, ym] = jnp.where(radial == 3, turn(above, 3 - ym), turn(own, 7))
                diagonal = turn(below, -ym) + is1 * float(DN[4, 4] ** 2) * own
                kdzj[xm, ym] = jnp.where(radial == 0, diagonal, 0.0)
            ends = [kzj[xm, zm] for zm in range(4)] + [arrived]
            scaled = [ends[i] * float(DN[i, 4]) for i in range(5)]
            for m in range(4):
                kzj[xm, m] = sum(scaled[i] * float(DN[i, m]) for i in range(5))
        send_z(0, j)

    def advance(j, t, first):
        z_copy(t - 1, j).wait_recv()
        uj, gxj, gyj, gzj, uyj = u.at[j], gx.at[j], gy.at[j], gz.at[j], uy.at[j]
        gy4j, gz4j, kdzj, zhj = gy4.at[j], gz4.at[j], kdz.at[j], zh.at[t - 1, j]
        imj, sfj, wj, hsj = im.at[j], sf.at[j], w.at[j], hs.at[j]

        for xm in range(4):
            x = 4 * j + xm
            if first:
                for zm in range(4):
                    if xm % 2 == 0:
                        masses = apart(strided(rows_m, 16 * x + zm, 512))
                        for ym in range(4):
                            mass = masses[ym] * (TIME_STEP * TIME_STEP)
                            one, two = twice_events(mass)
                            imj[xm, 4 * zm + ym], imj[xm + 1, 4 * zm + ym] = one, two
                    values = apart(strided(rows_v, 32 * x + zm, 1024))
                    for ym in range(4):
                        wj[xm, 4 * zm + ym] = values[ym] * TIME_STEP
                    values = apart(strided(rows_s, 32 * x + zm, 1024))
                    for ym in range(4):
                        sfj[xm, 4 * zm + ym] = values[ym] * imj[xm, 4 * zm + ym]
            v = [[uj[xm, 4 * zm + ym] for ym in range(4)] for zm in range(4)]
            f = [[None] * 4 for _ in range(4)]
            arrived = zhj[xm]
            above, below = arrived * is0, arrived * is1
            for ym in range(4):
                u4 = jnp.where(radial == 3, turn(above, 3 - ym), turn(v[0][ym], 7))
                parts = line(
                    *[v[zm][ym] for zm in range(4)], u4,
                    *[gzj[xm, 4 * zm + ym] for zm in range(4)], gz4j[xm, ym],
                )
                carried = jnp.where(radial == 0, turn(below, -ym), turn(parts[4], 1))
                f[0][ym] = (parts[0] + carried) + kdzj[xm, ym] * v[0][ym]
                f[1][ym], f[3][ym] = parts[1], parts[3]
                f[2][ym] = -parts[2]
            for zm in range(4):
                parts = line(
                    *v[zm], uyj[xm, zm], *[gyj[xm, 4 * zm + ym] for ym in range(4)], gy4j[xm, zm]
                )
                fy[xm, zm] = parts[4]
                fs[xm, 4 * zm] = f[zm][0] + parts[0]
                fs[xm, 4 * zm + 1] = f[zm][1] + parts[1]
                fs[xm, 4 * zm + 2] = f[zm][2] - parts[2]
                fs[xm, 4 * zm + 3] = f[zm][3] + parts[3]

        for xm in range(4):
            for zm in range(4):
                fy[xm, zm] = lane_before(fy[xm, zm])

        strength = jnp.where(upper, time_ref[0, t - 1], time_ref[1, t - 1])
        ubn, pbj, kdxj, gxn = ub.at[t - 1, j + 1], pb.at[t - 1, j], kdx.at[j], gx.at[j + 1, 0]
        for k in range(16):
            v = [uj[i, k] for i in range(4)]
            parts = line(*v, ubn[k], *[gxj[i, k] for i in range(4)], gxn[k], last=False)
            f = [
                fs[0, k] + (parts[0] + (pbj[k] + kdxj[k] * v[0])),
                fs[1, k] + parts[1],
                fs[2, k] - parts[2],
                fs[3, k] + parts[3],
            ]
            for i in range(4):
                if k % 4 == 0:
                    f[i] = f[i] + fy[i, k // 4]
                kick = strength * sfj[i, k] - imj[i, k] * f[i]
                speed = wj[i, k] + kick
                wj[i, k] = speed
                moved = v[i] + speed
                uj[i, k] = moved
                hsj[i, k] = kick * kick if first else hsj[i, k] + kick * kick
                if k % 4 == 0:
                    uyj[i, k // 4] = next_lane(moved)

    def hand_on(j, t):
        send_z(t, j)
        uj, ubj = u.at[j], ub.at[t, j]
        for k in range(16):
            ubj[k] = uj[0, k]
        partial_x(t, j)

        @pl.when(j == 0)
        def _():
            u_copy(t).start()

        @pl.when(j == 7)
        def _():
            p_copy(t).start()

    def end_copy(j, k, e):
        at = pl.ds(4 * j, 4)
        return pltpu.make_async_copy(
            nat_u.at[k, at, e], end_ref.at[e, at, :, pl.ds(128 * k, 128)], end_sem
        )

    def finish(j):
        uj, hsj = u.at[j], hs.at[j]
        for half in range(2):
            for zm in range(4):
                for ym in range(4):
                    one, two = hsj[2 * half, 4 * zm + ym], hsj[2 * half + 1, 4 * zm + ym]
                    one = one + pltpu.roll(one, 4, 0)
                    two = two + pltpu.roll(two, 4, 0)
                    fs[half, 4 * zm + ym] = jnp.where(upper, one, two) * (100.0 / (4 * STEPS))
        for half in range(2):
            for zm in range(4):
                both = [fs[half, 4 * zm + ym] for ym in range(4)]
                for k, value in enumerate(together(both)):
                    first = 512 * k + 16 * (4 * j + 2 * half) + zm
                    rows_sent[pl.ds(first, 8, stride=4), :] = value
        h_copy(j).start()
        for xm in range(4):
            for zm in range(4):
                whole = together([uj[xm, 4 * zm + ym] for ym in range(4)])
                for k, value in enumerate(whole):
                    rows_u[pl.ds(1024 * k + 32 * (4 * j + xm) + zm, 8, stride=4), :] = value
        for k in range(4):
            for e in range(2):
                end_copy(j, k, e).start()

    wait_late()

    @pl.loop(0, len(ORDER))
    def _(n):
        j, t = [
            jnp.where(block == 0, digit(n, [task[i] for task in ORDER_OF_FIRST], 4), digit(n, [task[i] for task in ORDER], 4))
            for i in range(2)
        ]

        @pl.when(jnp.logical_and(late, n == jnp.where(block == 0, 4, 0)))
        def _():
            pl.semaphore_wait(ready, 1)
            u_copy(0).start()
            g_copy().start()

        @pl.when(t == 1)
        def _():
            @pl.when(j == 0)
            def _():
                layer_copy().wait_recv()
                for k in range(16):
                    own = gx[0, 0, k] * float(DN[4, 4])
                    pb[0, 0, k] = layer[3, k] + own * layer[4, k]
                    kdx[0, k] = layer[5, k] + own * float(DN[4, 4])

            @pl.when(j == 7)
            def _():
                u_copy(0).wait_recv()
                g_copy().wait_recv()
                next_coefs(7)

            advance(j, t, True)
            hand_on(j, t)

        @pl.when(t > 1)
        def _():
            @pl.when(j == 0)
            def _():
                p_copy(t - 1).wait_recv()

            @pl.when(j == 7)
            def _():
                u_copy(t - 1).wait_recv()

            advance(j, t, False)

            @pl.when(t < STEPS)
            def _():
                hand_on(j, t)

            @pl.when(t == STEPS)
            def _():
                finish(j)

    @pl.loop(0, 8)
    def _(n):
        j = jnp.where(
            block == 0, *[digit(n, [j for j, t in order if t == STEPS], 4) for order in (ORDER_OF_FIRST, ORDER)]
        )
        h_copy(j).wait_recv()
        for xm in range(4):
            x = 4 * j + xm
            for k in range(4):
                hessian_ref[x, :, pl.ds(128 * k, 128)] = sent[k, x] + got[k, x]

    u_copy(0).wait_send()
    g_copy().wait_send()
    layer_copy().wait_send()
    gz_copy(0, 8).wait_send()
    for t in range(1, 4):
        u_copy(t).wait_send()
        p_copy(t).wait_send()

    @pl.loop(0, 8)
    def _(j):
        h_copy(j).wait_send()

    pltpu.make_async_copy(zs, zs, zsend).wait()
    pltpu.make_async_copy(nat_u, nat_u, end_sem).wait()


def per_device(slabs, blocks, *arrays):
    anywhere = pl.BlockSpec(memory_space=pl.ANY)
    inside = pl.BlockSpec(memory_space=pltpu.VMEM)

    def tiles(*shape):
        return pltpu.VMEM((*shape, 8, 128), jnp.float32)

    field, natural = tiles(8, 4, 16), pltpu.VMEM((4, 32, 16, 128), jnp.float32)
    natural_events = pltpu.VMEM((4, 32, 2, 16, 128), jnp.float32)
    several = pltpu.SemaphoreType.DMA
    scratch = [
        natural_events, natural_events, natural_events,
        natural, natural, pltpu.VMEM((32, 512), jnp.int32),
        field, field, field, field, field,
        tiles(9, 4, 16), field, field,
        tiles(8, 4, 4), tiles(8, 4, 4), tiles(8, 4, 4),
        tiles(8, 4, 16), tiles(9, 16), tiles(8, 4, 4), tiles(8, 4, 4),
        tiles(4, 9, 16), tiles(4, 9, 16), tiles(4, 16), tiles(4, 4),
        tiles(4, 8, 4), tiles(4, 8, 4), tiles(8, 4), tiles(8, 4),
        tiles(6, 16), pltpu.VMEM((4, 32, 128), jnp.int32),
        natural, natural, pltpu.VMEM((8, 8, 128), jnp.int32),
        several((3, 3)), several, several, several((4, 8)),
        several, several, several, several,
        several((4,)), several((4,)), several((4,)), several((4,)),
        several, several, several((8,)), several((8,)),
        pltpu.SemaphoreType.REGULAR,
    ]
    results = pl.pallas_call(
        functools.partial(body, slabs, blocks),
        out_shape=(
            pltpu.VMEM((2, 32, 16, 512), jnp.float32),
            pltpu.VMEM((32, 16, 512), jnp.float32),
        ),
        in_specs=[anywhere] * 3 + [pl.BlockSpec(memory_space=pltpu.SMEM)] + [anywhere] * 3,
        out_specs=(inside, inside),
        scratch_shapes=scratch,
        compiler_params=pltpu.CompilerParams(
            collective_id=0, has_side_effects=True, vmem_limit_bytes=56 << 20
        ),
        name="adjoint_steps",
    )(*arrays)
    return pl.pallas_call(
        place_out,
        out_shape=(
            jax.ShapeDtypeStruct((2, 32, 16, 512), jnp.float32),
            jax.ShapeDtypeStruct((32, 16, 512), jnp.float32),
        ),
        in_specs=[anywhere] * 2,
        out_specs=(anywhere, anywhere),
        scratch_shapes=[several((6,))],
        name="place_out",
    )(*[pltpu.with_memory_space_constraint(result, pltpu.VMEM) for result in results])


def solution(mesh):
    in_specs = (
        P("event", "block", "slab", None),
        P("event", "block", "slab", None),
        P("event", "block", "slab", None),
        P("event", None),
        P("block", "slab", None),
        P("block", "slab", None),
        P("block", None),
    )
    out_specs = (P("event", "block", "slab", None), P("block", "slab", None))
    return jax.shard_map(
        functools.partial(per_device, mesh.shape["slab"], mesh.shape["block"]),
        mesh=mesh, in_specs=in_specs, out_specs=out_specs, check_vma=False,
    )
```
